512 devices in a mesh: pix: 32 (over y, x), chan: 16 (over z, core).
Axes of the slice: x: 4, y: 8, z: 8, core: 2. Of those that a mesh axis runs over, the one named last changes fastest.
Arguments:
- counts: float32 [131072, 2048], P('pix', 'chan'), may hold values from 0.1 to 200, as said below
- offset: float32 [2048], P('chan'), may hold values from -0.5 to 0.5
- loading: float32 [2048, 128], P('chan'), may hold values from -0.125 to 0.125
Outputs:
- grad_loading: float32 [2048, 128], P('chan')
- grad_offset: float32 [2048], P('chan')
The draws below stay inside these ranges and needn't reach their ends.
Inputs may be any that keep to these rules, and one draw needn't show every extreme that they name: counts are positive intensities.
All inputs are finite; a program needn't handle non-finite values.
Results may differ from the reference program's by a relative error of at most 0.00024.
Values sent between devices are 32-bit elements; how exact they have to be, the bound alone decides.
No kernel may reach another device: no remote copies, remote signals or barrier semaphores. Data moves between devices by JAX's collectives and lax.ppermute only.
A program may use at most 64 MiB of HBM per device.

```python
import jax
import jax.numpy as jnp
from jax import lax

CHANNELS = 2048
COMPONENTS = 128
PIXELS = 131072


def draw_counts(key, part):
    key = jax.random.fold_in(key, 7)
    rows = jnp.arange(PIXELS, dtype=jnp.float32)[:, None]
    spread = 0.4 + 0.8 * rows / PIXELS
    noise = jnp.clip(jax.random.normal(key, (PIXELS, CHANNELS), jnp.float32), -3.0, 3.0)
    return jnp.exp(1.5 + spread * noise)


def block_levels(key, shape, pieces, smallest, top_value):
    level = 1.0
    for position, parts in pieces:
        steps = jax.random.uniform(jax.random.fold_in(jax.random.fold_in(key, 6), position), (parts,), jnp.float32, smallest / len(pieces), top_value / len(pieces))
        level = level * jnp.repeat(jnp.exp(steps), shape[position] // parts).reshape((-1,) + (1,) * (len(shape) - 1 - position))
    return level


def gaussian(key, extent, width, reach, shards=(), held_as=jnp.bfloat16):
    gain = block_levels(key, extent, shards, -0.22, 0.18) if shards else 1.0
    array = jax.random.normal(key, extent, jnp.float32) * width * gain
    return jnp.minimum(jnp.maximum(array, -reach), reach).astype(held_as)


def setup_inputs(seed: int = 0) -> dict:
    splits = jax.random.split(jax.random.key(seed), 4)
    counts = draw_counts(jax.random.fold_in(splits[3], 71), 0)
    offset = jnp.clip(jax.random.uniform(splits[1], (CHANNELS,), jnp.float32, -0.5, 0.5) * block_levels(splits[1], (CHANNELS,), ((0, 16),), -0.4, 0.0), -0.5, 0.5)
    loading = gaussian(splits[2], (CHANNELS, COMPONENTS), CHANNELS ** -0.5, 0.125, ((0, 16),), jnp.float32)
    return dict(counts=counts, offset=offset, loading=loading)


def mult(a, b):
    return jnp.dot(a, b, preferred_element_type=jnp.float32, precision=lax.Precision.HIGHEST)


def reference(counts, offset, loading):
    logs = jnp.log(counts)
    geo = jnp.mean(logs, axis=1, keepdims=True)
    centred = logs - geo - offset[None, :]
    scores = mult(centred, loading)
    err = mult(scores, loading.T) - centred
    back = mult(err, loading)
    grad_loading = (mult(centred.T, back) + mult(err.T, scores)) / PIXELS
    grad_offset = -jnp.sum(mult(back, loading.T) - err, axis=0) / PIXELS
    return grad_loading, grad_offset
```

```python
import functools

import jax
import jax.numpy as jnp
from jax import lax
from jax.experimental import pallas as pl
from jax.experimental.pallas import tpu as pltpu
from jax.sharding import Mesh
from jax.sharding import PartitionSpec as P

F32 = jnp.float32
WIDE = ("y", "x")
DEEP = ("z", "c")
LIMIT = 48 * 1024 * 1024


def mult(left, right, contract=((1,), (0,))):
    return lax.dot_general(
        left, right, (contract, ((), ())),
        preferred_element_type=F32, precision=lax.Precision.HIGHEST,
    )


def whole(shape):
    return jax.ShapeDtypeStruct(shape, F32)


def call(body, out_shape, *args):
    return pl.pallas_call(
        body,
        out_shape=out_shape,
        compiler_params=pltpu.CompilerParams(vmem_limit_bytes=LIMIT),
    )(*args)


def send_body(which_ref, counts_ref, loading_ref, offset_ref, out_ref):
    half, comps = counts_ref.shape[0], loading_ref.shape[0]
    out_ref[0:half, :] = jnp.log(counts_ref[...])
    out_ref[half : half + comps, :] = loading_ref[...]
    out_ref[half + comps : half + comps + 8, :] = jnp.broadcast_to(offset_ref[...], (8, comps))


def keep_body(which_ref, counts_ref, out_ref):
    out_ref[...] = jnp.log(counts_ref[...])


def half_spec(half, width):
    return pl.BlockSpec((half, width), lambda i, which: (which[0], 0))


def on_half(body, which, counts, others, rows):
    half, width = counts.shape[0] // 2, counts.shape[1]
    specs = [half_spec(half, width)]
    specs += [pl.BlockSpec(a.shape, lambda i, which: (0, 0)) for a in others]
    return pl.pallas_call(
        body,
        out_shape=whole((rows, width)),
        grid_spec=pltpu.PrefetchScalarGridSpec(
            num_scalar_prefetch=1,
            grid=(1,),
            in_specs=specs,
            out_specs=pl.BlockSpec((rows, width), lambda i, which: (0, 0)),
        ),
        compiler_params=pltpu.CompilerParams(vmem_limit_bytes=LIMIT),
    )(which, counts, *others)


def encode_body(parts, mine_ref, other_ref, loading_ref, offset_ref, out_ref):
    half, comps = mine_ref.shape
    rows, share = half // parts, comps // parts
    mine = loading_ref[...]
    other = other_ref[half : half + comps, :]
    bar_mine = jnp.sum(mine, axis=0, keepdims=True) / comps
    bar_other = jnp.sum(other, axis=0, keepdims=True) / comps
    mine_c, other_c = mine - bar_mine, other - bar_other
    shift = mult(jnp.broadcast_to(offset_ref[...], (8, comps)), mine)
    shift += mult(other_ref[half + comps : half + comps + 8, :], other)
    gram = mult(mine, mine, ((0,), (0,))) + mult(other, other, ((0,), (0,)))
    ones = jnp.ones((8, comps), F32)
    for j in range(parts):
        a = mine_ref[j * rows : (j + 1) * rows, :]
        b = other_ref[j * rows : (j + 1) * rows, :]
        out_ref[j, 0:rows, :] = mult(a, mine_c) + mult(b, other_c)
        for h in range(rows // comps):
            sums = mult(ones, a[h * comps : (h + 1) * comps, :], ((1,), (1,)))
            out_ref[j, rows + h : rows + h + 1, :] = sums[0:1, :]
            sums = mult(ones, b[h * comps : (h + 1) * comps, :], ((1,), (1,)))
            out_ref[j, rows + 2 + h : rows + 3 + h, :] = sums[0:1, :]
        out_ref[j, rows + 4 : rows + 5, :] = bar_mine
        out_ref[j, rows + 5 : rows + 6, :] = bar_other
        out_ref[j, rows + 6 : rows + 7, :] = shift[0:1, :]
        out_ref[j, rows + 7 : rows + 8, :] = jnp.zeros((1, comps), F32)
        out_ref[j, rows + 8 : rows + 8 + share, :] = gram[j * share : (j + 1) * share, :]


def finish_body(channels, in_ref, out_ref):
    parts, height, comps = in_ref.shape
    share = comps // parts
    rows = height - 8 - share
    bars = jnp.concatenate([in_ref[j, rows + 4 : rows + 6, :] for j in range(parts)], axis=0)
    shift = in_ref[0, rows + 6 : rows + 7, :]
    for j in range(1, parts):
        shift += in_ref[j, rows + 6 : rows + 7, :]
    for h in range(rows // comps):
        sums = jnp.concatenate(
            [
                in_ref[j, rows + 2 * k + h : rows + 2 * k + h + 1, :]
                for j in range(parts)
                for k in range(2)
            ],
            axis=0,
        )
        geo = jnp.sum(sums, axis=0, keepdims=True) / channels
        apart = sums - comps * geo
        at = h * comps
        total = mult(apart, bars, ((0,), (0,))) - shift
        for j in range(parts):
            total += in_ref[j, at : at + comps, :]
        for j in range(parts):
            out_ref[j, at : at + comps, :] = total
            out_ref[j, rows + h : rows + h + 1, :] = geo
    gram = in_ref[0, rows + 8 : rows + 8 + share, :]
    for j in range(1, parts):
        gram += in_ref[j, rows + 8 : rows + 8 + share, :]
    for j in range(parts):
        out_ref[j, rows + 2 : rows + 8, :] = jnp.zeros((6, comps), F32)
        out_ref[j, rows + 8 : rows + 8 + share, :] = gram


def grad_body(in_ref, mine_ref, other_ref, loading_ref, offset_ref, mine_out, other_out):
    parts, height, comps = in_ref.shape
    share = comps // parts
    rows = height - 8 - share
    half = parts * rows
    gram = jnp.concatenate([in_ref[j, rows + 8 : rows + 8 + share, :] for j in range(parts)], axis=0)
    row = lax.broadcasted_iota(jnp.int32, (comps, comps), 0)
    col = lax.broadcasted_iota(jnp.int32, (comps, comps), 1)
    hat = gram - jnp.where(row == col, 2.0, 0.0).astype(F32)
    mine_l = loading_ref[...]
    other_l = other_ref[half : half + comps, :]
    mine_off = offset_ref[...]
    other_off = other_ref[half + comps : half + comps + 1, :]
    pick = lax.broadcasted_iota(jnp.int32, (8, comps), 0)
    zero = jnp.zeros((comps, comps), F32)
    w_mine, w_other, square = zero, zero, zero
    s_sum = jnp.zeros((1, comps), F32)
    c_mine, c_other = s_sum, s_sum
    for j in range(parts):
        geos = in_ref[j, rows : rows + 8, :]
        for h in range(rows // comps):
            at = j * rows + h * comps
            s = in_ref[j, h * comps : (h + 1) * comps, :]
            geo = mult(geos, jnp.where(pick == h, 1.0, 0.0).astype(F32), ((0,), (0,)))
            a = mine_ref[at : at + comps, :] - geo - mine_off
            b = other_ref[at : at + comps, :] - geo - other_off
            turned = s.T
            w_mine += mult(turned, a)
            w_other += mult(turned, b)
            square += mult(turned, s)
            s_sum += jnp.sum(s, axis=0, keepdims=True)
            c_mine += jnp.sum(a, axis=0, keepdims=True)
            c_other += jnp.sum(b, axis=0, keepdims=True)
    s_hat = mult(jnp.broadcast_to(s_sum, (8, comps)), hat)
    for w, load, c, out in ((w_mine, mine_l, c_mine, mine_out), (w_other, other_l, c_other, other_out)):
        out[0:comps, :] = mult(w.T, hat) + mult(load, square)
        out[comps : comps + 8, :] = -(mult(s_hat, load, ((1,), (1,))) + c)


def add_body(a_ref, b_ref, out_ref):
    total = a_ref[...] + b_ref[...]
    for j in range(out_ref.shape[0]):
        out_ref[j] = total


def gather_body(in_ref, out_ref):
    total = jnp.sum(in_ref[...], axis=0)
    for j in range(out_ref.shape[0]):
        out_ref[j] = total


def last_body(pixels, in_ref, load_ref, off_ref):
    comps = load_ref.shape[0]
    total = jnp.sum(in_ref[...], axis=0) / pixels
    load_ref[...] = total[0:comps, :]
    off_ref[...] = total[comps : comps + 1, :]


def on_device(counts, offset, loading):
    pixels = counts.shape[0] * lax.axis_size(WIDE)
    comps = loading.shape[1]
    parts = lax.axis_size("z")
    channels = counts.shape[1] * parts * 2
    half = counts.shape[0] // 2
    rows = half // parts
    height = rows + 8 + comps // parts
    core = lax.axis_index("c").astype(jnp.int32)
    offset = offset.reshape(1, comps)

    sent = on_half(send_body, (1 - core).reshape(1), counts, (loading, offset), half + comps + 8)
    other = lax.ppermute(sent, "c", [(0, 1), (1, 0)])
    mine = on_half(keep_body, core.reshape(1), counts, (), half)
    partial = call(
        functools.partial(encode_body, parts), whole((parts, height, comps)), mine, other, loading, offset
    )
    gathered = lax.all_to_all(partial, "z", 0, 0)
    copies = call(functools.partial(finish_body, channels), whole((parts, height, comps)), gathered)
    scores = lax.all_to_all(copies, "z", 0, 0)
    shape = whole((comps + 8, comps))
    grad_mine, grad_other = call(grad_body, (shape, shape), scores, mine, other, loading, offset)
    arrived = lax.ppermute(grad_other, "c", [(0, 1), (1, 0)])
    nx, ny = lax.axis_size("x"), lax.axis_size("y")
    total = call(add_body, whole((nx, comps + 8, comps)), grad_mine, arrived)
    total = lax.all_to_all(total, "x", 0, 0)
    total = call(gather_body, whole((ny, comps + 8, comps)), total)
    total = lax.all_to_all(total, "y", 0, 0)
    grad, grad_offset = call(
        functools.partial(last_body, pixels), (whole((comps, comps)), whole((1, comps))), total
    )
    return grad, grad_offset.reshape(comps)


def solution(mesh):
    wide, deep = mesh.devices.shape
    split = Mesh(mesh.devices.reshape(wide // 4, 4, deep // 2, 2), WIDE + DEEP)
    return jax.shard_map(
        on_device,
        mesh=split,
        in_specs=(P(WIDE, DEEP), P(DEEP), P(DEEP, None)),
        out_specs=(P(DEEP, None), P(DEEP)),
        check_vma=False,
    )
```

```python
import functools

import jax
import jax.numpy as jnp
from jax import lax
from jax.experimental import pallas as pl
from jax.experimental.pallas import tpu as pltpu
from jax.sharding import Mesh
from jax.sharding import PartitionSpec as P

F32 = jnp.float32
AXES = ("y", "x", "zh", "zl", "c")
WIDE = ("y", "x")
DEEP = ("zh", "zl", "c")
LIMIT = 48 * 1024 * 1024


def mult(left, right, contract=((1,), (0,))):
    return lax.dot_general(
        left, right, (contract, ((), ())),
        preferred_element_type=F32, precision=lax.Precision.HIGHEST,
    )


def whole(*shape):
    return jax.ShapeDtypeStruct(shape, F32)


def call(body, out_shape, *args):
    return pl.pallas_call(
        body,
        out_shape=out_shape,
        compiler_params=pltpu.CompilerParams(vmem_limit_bytes=LIMIT),
    )(*args)


def tail(loading_ref, offset_ref, out_ref):
    comps = loading_ref.shape[0]
    rows = out_ref.shape[0] - comps - 8
    out_ref[rows : rows + comps, :] = loading_ref[...]
    out_ref[rows + comps : rows + comps + 8, :] = jnp.broadcast_to(offset_ref[...], (8, comps))
    return rows


def split_body(which, keep_in, core_in, near_in, far_in, loading_ref, offset_ref, keep, core, near, far):
    rows = tail(loading_ref, offset_ref, near)
    near[0:rows, :] = jnp.log(near_in[...])
    tail(loading_ref, offset_ref, far)
    far[0:rows, :] = jnp.log(far_in[...])
    core[...] = jnp.log(core_in[...])
    keep[...] = jnp.log(keep_in[...])


def split(which, counts, loading, offset):
    rows, width = counts.shape[0] // 4, counts.shape[1]

    def block(k):
        return pl.BlockSpec((rows, width), lambda i, which: (which[k], 0))

    def full(shape):
        return pl.BlockSpec(shape, lambda i, which: (0, 0))

    more = rows + loading.shape[0] + 8
    heights = (rows, rows, more, more)
    return pl.pallas_call(
        split_body,
        out_shape=tuple(whole(h, width) for h in heights),
        grid_spec=pltpu.PrefetchScalarGridSpec(
            num_scalar_prefetch=1,
            grid=(1,),
            in_specs=[block(k) for k in range(4)] + [full(loading.shape), full(offset.shape)],
            out_specs=tuple(full((h, width)) for h in heights),
        ),
        compiler_params=pltpu.CompilerParams(vmem_limit_bytes=LIMIT),
    )(which, counts, counts, counts, counts, loading, offset)


def log_sums(logs, ones, comps):
    return [
        mult(ones, logs[h * comps : (h + 1) * comps, :], ((1,), (1,)))[0:1, :]
        for h in range(logs.shape[0] // comps)
    ]


def encode_body(parts, keep, core, near, far, loading_ref, out_ref):
    total, comps = keep.shape
    rows, share = total // parts, comps // parts
    loads = [loading_ref[...], far[total : total + comps, :], near[total : total + comps, :]]
    bars = [jnp.sum(load, axis=0, keepdims=True) / comps for load in loads]
    bare = [load - bar for load, bar in zip(loads, bars)]
    pair = jnp.concatenate(bare[0:2], axis=0)
    gram = mult(loads[0], loads[0], ((0,), (0,)))
    for load in loads[1:]:
        gram += mult(load, load, ((0,), (0,)))
    shift = mult(far[total + comps : total + comps + 8, :], loads[1])
    shift += mult(near[total + comps : total + comps + 8, :], loads[2])
    ones = jnp.ones((8, comps), F32)
    for j in range(parts):
        logs = [source[j * rows : (j + 1) * rows, :] for source in (keep, core, near)]
        both = jnp.concatenate(logs[0:2], axis=1)
        out_ref[j, 0:rows, :] = mult(both, pair) + mult(logs[2], bare[2])
        for k, part in enumerate(logs):
            for h, sums in enumerate(log_sums(part, ones, comps)):
                at = rows + 4 * h + k
                out_ref[j, at : at + 1, :] = sums
            out_ref[j, rows + 8 + k : rows + 9 + k, :] = bars[k]
        out_ref[j, rows + 12 : rows + 13, :] = shift[0:1, :]
        out_ref[j, rows + 16 : rows + 16 + share, :] = gram[j * share : (j + 1) * share, :]


def encode_last_body(in_ref, more, loading_ref, offset_ref, out_ref):
    parts, height, comps = in_ref.shape
    share = comps // parts
    rows = height - 16 - share
    total = parts * rows
    load = more[total : total + comps, :]
    bar = jnp.sum(load, axis=0, keepdims=True) / comps
    bare = load - bar
    gram = mult(load, load, ((0,), (0,)))
    shift = mult(more[total + comps : total + comps + 8, :], load)
    shift += mult(jnp.broadcast_to(offset_ref[...], (8, comps)), loading_ref[...])
    ones = jnp.ones((8, comps), F32)
    blank = jnp.zeros((3, comps), F32)
    for j in range(parts):
        logs = more[j * rows : (j + 1) * rows, :]
        out_ref[j, 0:rows, :] = in_ref[j, 0:rows, :] + mult(logs, bare)
        for h, sums in enumerate(log_sums(logs, ones, comps)):
            at = rows + 4 * h
            out_ref[j, at : at + 3, :] = in_ref[j, at : at + 3, :]
            out_ref[j, at + 3 : at + 4, :] = sums
        out_ref[j, rows + 8 : rows + 11, :] = in_ref[j, rows + 8 : rows + 11, :]
        out_ref[j, rows + 11 : rows + 12, :] = bar
        out_ref[j, rows + 12 : rows + 13, :] = in_ref[j, rows + 12 : rows + 13, :] + shift[0:1, :]
        out_ref[j, rows + 13 : rows + 16, :] = blank
        at = rows + 16
        out_ref[j, at : at + share, :] = in_ref[j, at : at + share, :] + gram[j * share : (j + 1) * share, :]


def finish_body(channels, in_ref, out_ref):
    parts, height, comps = in_ref.shape
    share = comps // parts
    rows = height - 16 - share
    bars = jnp.concatenate([in_ref[j, rows + 8 : rows + 12, :] for j in range(parts)], axis=0)
    shift = in_ref[0, rows + 12 : rows + 13, :]
    for j in range(1, parts):
        shift += in_ref[j, rows + 12 : rows + 13, :]
    for h in range(rows // comps):
        sums = jnp.concatenate(
            [in_ref[j, rows + 4 * h : rows + 4 * h + 4, :] for j in range(parts)], axis=0
        )
        geo = jnp.sum(sums, axis=0, keepdims=True) / channels
        at = h * comps
        total = mult(sums - comps * geo, bars, ((0,), (0,))) - shift
        for j in range(parts):
            total += in_ref[j, at : at + comps, :]
        for j in range(parts):
            out_ref[j, at : at + comps, :] = total
            out_ref[j, rows + h : rows + h + 1, :] = geo
    gram = in_ref[0, rows + 16 : rows + 16 + share, :]
    for j in range(1, parts):
        gram += in_ref[j, rows + 16 : rows + 16 + share, :]
    for j in range(parts):
        out_ref[j, rows + 2 : rows + 8, :] = jnp.zeros((6, comps), F32)
        out_ref[j, rows + 8 : rows + 8 + share, :] = gram


def grad_body(in_ref, keep, core, near, far, more, loading_ref, offset_ref, mine_out, near_out):
    parts, height, comps = in_ref.shape
    share = comps // parts
    rows = height - 8 - share
    total = parts * rows
    gram = jnp.concatenate([in_ref[j, rows + 8 : rows + 8 + share, :] for j in range(parts)], axis=0)
    row = lax.broadcasted_iota(jnp.int32, (comps, comps), 0)
    col = lax.broadcasted_iota(jnp.int32, (comps, comps), 1)
    hat = gram - jnp.where(row == col, 2.0, 0.0).astype(F32)
    logs = (keep, core, near, more)
    loads = (loading_ref[...],) + tuple(a[total : total + comps, :] for a in (far, near, more))
    offs = (offset_ref[...],) + tuple(a[total + comps : total + comps + 1, :] for a in (far, near, more))
    pick = lax.broadcasted_iota(jnp.int32, (8, comps), 0)
    wide = jnp.zeros((comps, 5 * comps), F32)
    s_sum = jnp.zeros((1, comps), F32)
    c_sum = [s_sum] * 4
    for j in range(parts):
        geos = in_ref[j, rows : rows + 8, :]
        s = in_ref[j, 0:rows, :]
        s_sum += jnp.sum(s, axis=0, keepdims=True)
        geo = jnp.concatenate(
            [
                mult(geos, jnp.where(pick == h, 1.0, 0.0).astype(F32), ((0,), (0,)))
                for h in range(rows // comps)
            ],
            axis=0,
        )
        centred = [a[j * rows : (j + 1) * rows, :] - geo - off for a, off in zip(logs, offs)]
        c_sum = [c + jnp.sum(a, axis=0, keepdims=True) for c, a in zip(c_sum, centred)]
        wide += mult(s.T, jnp.concatenate(centred + [s], axis=1))
    square = wide[:, 4 * comps : 5 * comps]
    s_hat = mult(jnp.broadcast_to(s_sum, (8, comps)), hat)
    for k in range(4):
        out = (mine_out, near_out)[k // 2]
        w = wide[:, k * comps : (k + 1) * comps]
        out[k % 2, 0:comps, :] = mult(w.T, hat) + mult(loads[k], square)
        out[k % 2, comps : comps + 8, :] = -(mult(s_hat, loads[k], ((1,), (1,))) + c_sum[k])


def deal_body(which, a_ref, b_ref, out_ref):
    core = which[0]
    _, height, comps = a_ref.shape
    pieces = out_ref.shape[0] // 2
    share = comps // pieces
    sums = [a_ref[k] + b_ref[k] for k in range(2)]
    for p in range(pieces):
        for k in range(2):
            first, other = sums[k], sums[1 - k]
            for rows, at in ((slice(p * share, (p + 1) * share), 0), (slice(comps, comps + 8 - share), share)):
                piece = jnp.where(core == 0, first[rows, :], other[rows, :])
                out_ref[2 * p + k, at : at + piece.shape[0], :] = piece


def deal(which, a, b, devices):
    comps = a.shape[2]
    return pl.pallas_call(
        deal_body,
        out_shape=whole(devices, 8, comps),
        in_specs=[
            pl.BlockSpec(memory_space=pltpu.SMEM),
            pl.BlockSpec(memory_space=pltpu.VMEM),
            pl.BlockSpec(memory_space=pltpu.VMEM),
        ],
        compiler_params=pltpu.CompilerParams(vmem_limit_bytes=LIMIT),
    )(which, a, b)


def gather_body(pixels, in_ref, out_ref):
    total = jnp.sum(in_ref[...], axis=0) / pixels
    for j in range(out_ref.shape[0]):
        out_ref[j] = total


def last_body(in_ref, load_ref, off_ref):
    pieces = in_ref.shape[0]
    share = load_ref.shape[0] // pieces
    for p in range(pieces):
        load_ref[p * share : (p + 1) * share, :] = in_ref[p, 0:share, :]
    off_ref[...] = in_ref[0, share : share + 1, :]


def on_device(counts, offset, loading):
    pixels = counts.shape[0] * lax.axis_size(WIDE)
    comps = loading.shape[1]
    parts = lax.axis_size("zh")
    channels = counts.shape[1] * parts * 4
    rows = counts.shape[0] // 4 // parts
    share = comps // parts
    core = lax.axis_index("c").astype(jnp.int32)
    side = lax.axis_index("zl").astype(jnp.int32)
    which = jnp.stack(
        [2 * core + side, 2 * (1 - core) + side, 2 * core + 1 - side, 2 * (1 - core) + 1 - side]
    )
    offset = offset.reshape(1, comps)

    swap = [(0, 1), (1, 0)]
    z_size = 2 * parts
    near_pairs = []
    for z in range(z_size):
        for c in range(2):
            partner = (((z - c) % z_size ^ 1) + c) % z_size
            near_pairs.append((2 * z + c, 2 * partner + c))

    keep, core_out, near_out, far_out = split(which, counts, loading, offset)
    near = lax.ppermute(near_out, DEEP, near_pairs)
    far = lax.ppermute(far_out, "c", swap)
    more = lax.ppermute(far, DEEP, near_pairs)
    other = lax.ppermute(core_out, "c", swap)
    height = rows + 16 + share
    partial = call(
        functools.partial(encode_body, parts), whole(parts, height, comps), keep, other, near, far, loading
    )
    partial = call(encode_last_body, whole(parts, height, comps), partial, more, loading, offset)
    gathered = lax.all_to_all(partial, "zh", 0, 0)
    copies = call(functools.partial(finish_body, channels), whole(parts, height - 8, comps), gathered)
    scores = lax.all_to_all(copies, "zh", 0, 0)
    shape = whole(2, comps + 8, comps)
    grad_mine, grad_near = call(
        grad_body, (shape, shape), scores, keep, other, near, far, more, loading, offset
    )
    arrived = lax.ppermute(grad_near, DEEP, near_pairs)
    plane = lax.axis_size(WIDE)
    pieces = deal(core.reshape(1), grad_mine, arrived, 2 * plane)
    pieces = lax.all_to_all(pieces, WIDE + ("c",), 0, 0)
    pieces = call(functools.partial(gather_body, pixels), whole(plane, 8, comps), pieces)
    pieces = lax.all_to_all(pieces, WIDE, 0, 0)
    grad, grad_offset = call(last_body, (whole(comps, comps), whole(1, comps)), pieces)
    return grad, grad_offset.reshape(comps)


def solution(mesh):
    wide, deep = mesh.devices.shape
    split_mesh = Mesh(mesh.devices.reshape(wide // 4, 4, deep // 4, 2, 2), AXES)
    return jax.shard_map(
        on_device,
        mesh=split_mesh,
        in_specs=(P(WIDE, DEEP), P(DEEP), P(DEEP, None)),
        out_specs=(P(DEEP, None), P(DEEP)),
        check_vma=False,
    )
```

```python
import functools

import jax
import jax.numpy as jnp
from jax import lax
from jax.experimental import pallas as pl
from jax.experimental.pallas import tpu as pltpu
from jax.sharding import Mesh
from jax.sharding import PartitionSpec as P

F32 = jnp.float32
AXES = ("y", "x", "zh", "zl", "c")
WIDE = ("y", "x")
DEEP = ("zh", "zl", "c")
PARTS = 4
LIMIT = 48 * 1024 * 1024
EDGE = 48 * 1024 * 1024


def mult(left, right, contract=((1,), (0,))):
    return lax.dot_general(
        left, right, (contract, ((), ())),
        preferred_element_type=F32, precision=lax.Precision.HIGHEST,
    )


def whole(*shape):
    return jax.ShapeDtypeStruct(shape, F32)


def call(body, out_shape, *args, scalars=0):
    spaces = [pltpu.SMEM] * scalars + [pltpu.VMEM] * (len(args) - scalars)
    return pl.pallas_call(
        body,
        out_shape=out_shape,
        in_specs=[pl.BlockSpec(memory_space=space) for space in spaces],
        compiler_params=pltpu.CompilerParams(vmem_limit_bytes=LIMIT),
    )(*args)


def cut_body(which, counts_ref, out_ref):
    out_ref[...] = jnp.log(counts_ref[...])


def cut_more_body(which, counts_ref, loading_ref, offset_ref, out_ref):
    rows, comps = counts_ref.shape
    out_ref[0:rows, :] = jnp.log(counts_ref[...])
    out_ref[rows : rows + comps, :] = loading_ref[...]
    out_ref[rows + comps : rows + comps + 8, :] = jnp.broadcast_to(offset_ref[...], (8, comps))


def cut(which, counts, *others):
    rows, width = counts.shape[0] // 4, counts.shape[1]

    def full(shape):
        return pl.BlockSpec(shape, lambda i, which: (0, 0))

    height = rows + (others[0].shape[0] + 8 if others else 0)
    return pl.pallas_call(
        cut_more_body if others else cut_body,
        out_shape=whole(height, width),
        grid_spec=pltpu.PrefetchScalarGridSpec(
            num_scalar_prefetch=1,
            grid=(1,),
            in_specs=[pl.BlockSpec((rows, width), lambda i, which: (which[0], 0))]
            + [full(a.shape) for a in others],
            out_specs=full((height, width)),
        ),
        compiler_params=pltpu.CompilerParams(vmem_limit_bytes=EDGE),
    )(which.reshape(1), counts, *others)


def log_sums(logs, ones, comps):
    return [
        mult(ones, logs[h * comps : (h + 1) * comps, :], ((1,), (1,)))[0:1, :]
        for h in range(logs.shape[0] // comps)
    ]


def encode_body(keep, core, near, far, loading_ref, out_ref):
    total, comps = keep.shape
    parts = PARTS
    rows, share = total // parts, comps // parts
    loads = [loading_ref[...], far[total : total + comps, :], near[total : total + comps, :]]
    bars = [jnp.sum(load, axis=0, keepdims=True) / comps for load in loads]
    bare = [load - bar for load, bar in zip(loads, bars)]
    pair = jnp.concatenate(bare[0:2], axis=0)
    gram = mult(loads[0], loads[0], ((0,), (0,)))
    for load in loads[1:]:
        gram += mult(load, load, ((0,), (0,)))
    shift = mult(far[total + comps : total + comps + 8, :], loads[1])
    shift += mult(near[total + comps : total + comps + 8, :], loads[2])
    ones = jnp.ones((8, comps), F32)
    for j in range(parts):
        logs = [source[j * rows : (j + 1) * rows, :] for source in (keep, core, near)]
        both = jnp.concatenate(logs[0:2], axis=1)
        out_ref[j, 0:rows, :] = mult(both, pair) + mult(logs[2], bare[2])
        for k, part in enumerate(logs):
            for h, sums in enumerate(log_sums(part, ones, comps)):
                at = rows + 4 * h + k
                out_ref[j, at : at + 1, :] = sums
            out_ref[j, rows + 8 + k : rows + 9 + k, :] = bars[k]
        out_ref[j, rows + 12 : rows + 13, :] = shift[0:1, :]
        out_ref[j, rows + 16 : rows + 16 + share, :] = gram[j * share : (j + 1) * share, :]


def encode_last_body(steps, place, in_ref, more, loading_ref, offset_ref, *outs):
    parts, height, comps = in_ref.shape
    share = comps // parts
    rows = height - 16 - share
    total = parts * rows
    load = more[total : total + comps, :]
    bar = jnp.sum(load, axis=0, keepdims=True) / comps
    bare = load - bar
    gram = mult(load, load, ((0,), (0,)))
    shift = mult(more[total + comps : total + comps + 8, :], load)
    shift += mult(jnp.broadcast_to(offset_ref[...], (8, comps)), loading_ref[...])
    ones = jnp.ones((8, comps), F32)
    blank = jnp.zeros((3, comps), F32)
    for step, out_ref in zip(steps, outs):
        j = lax.rem(place[0] + step, parts)
        logs = more[pl.ds(pl.multiple_of(j * rows, rows), rows), :]
        out_ref[0:rows, :] = in_ref[j, 0:rows, :] + mult(logs, bare)
        for h, sums in enumerate(log_sums(logs, ones, comps)):
            at = rows + 4 * h
            out_ref[at : at + 3, :] = in_ref[j, at : at + 3, :]
            out_ref[at + 3 : at + 4, :] = sums
        out_ref[rows + 8 : rows + 11, :] = in_ref[j, rows + 8 : rows + 11, :]
        out_ref[rows + 11 : rows + 12, :] = bar
        out_ref[rows + 12 : rows + 13, :] = in_ref[j, rows + 12 : rows + 13, :] + shift[0:1, :]
        out_ref[rows + 13 : rows + 16, :] = blank
        at = rows + 16
        mine = in_ref[j, at : at + share, :]
        for q in range(parts):
            mine += jnp.where(j == q, gram[q * share : (q + 1) * share, :], 0.0)
        out_ref[at : at + share, :] = mine


def finish_body(channels, *refs):
    ins, out_ref = refs[:-1], refs[-1]
    parts = len(ins)
    height, comps = ins[0].shape
    share = comps // parts
    rows = height - 16 - share
    bars = jnp.concatenate([a[rows + 8 : rows + 12, :] for a in ins], axis=0)
    shift = sum(a[rows + 12 : rows + 13, :] for a in ins)
    for h in range(rows // comps):
        sums = jnp.concatenate([a[rows + 4 * h : rows + 4 * h + 4, :] for a in ins], axis=0)
        geo = jnp.sum(sums, axis=0, keepdims=True) / channels
        at = h * comps
        total = mult(sums - comps * geo, bars, ((0,), (0,))) - shift
        for a in ins:
            total += a[at : at + comps, :]
        out_ref[at : at + comps, :] = total
        out_ref[rows + h : rows + h + 1, :] = geo
    out_ref[rows + 2 : rows + 8, :] = jnp.zeros((6, comps), F32)
    out_ref[rows + 8 : rows + 8 + share, :] = sum(a[rows + 16 : rows + 16 + share, :] for a in ins)


def block_terms(j, s_ref, logs, offs, rows):
    comps = s_ref.shape[1]
    pick = lax.broadcasted_iota(jnp.int32, (8, comps), 0)
    geos = s_ref[rows : rows + 8, :]
    s = s_ref[0:rows, :]
    geo = jnp.concatenate(
        [
            mult(geos, jnp.where(pick == h, 1.0, 0.0).astype(F32), ((0,), (0,)))
            for h in range(rows // comps)
        ],
        axis=0,
    )
    here = pl.ds(pl.multiple_of(j * rows, rows), rows)
    both = jnp.concatenate([a[here, :] - geo - off for a, off in zip(logs, offs)] + [s], axis=1)
    return mult(s.T, both), jnp.sum(both, axis=0, keepdims=True)


def grad_body(steps, place, keep, core, near, far, more, offset_ref, *refs):
    total, comps = keep.shape
    out_ref = refs[-1]
    blocks, before = refs[: len(steps)], refs[len(steps) : -1]
    parts = PARTS
    rows = total // parts
    logs = (keep, core, near, more)
    offs = (offset_ref[...],) + tuple(a[total + comps : total + comps + 1, :] for a in (far, near, more))
    wide, sums = 0.0, 0.0
    if before:
        wide, sums = before[0][0:comps, :], before[0][comps : comps + 1, :]
    for step, block in zip(steps, blocks):
        j = lax.rem(place[0] + parts - step, parts)
        more_wide, more_sums = block_terms(j, block, logs, offs, rows)
        wide, sums = wide + more_wide, sums + more_sums
    out_ref[0:comps, :] = wide
    out_ref[comps : comps + 8, :] = jnp.broadcast_to(sums, (8, sums.shape[1]))


def last_grad_body(place, in_ref, near, far, more, loading_ref, own, one, two, three, *outs):
    comps = loading_ref.shape[0]
    total = near.shape[0] - comps - 8
    share = comps // PARTS
    rows = own.shape[0] - 8 - share
    row = lax.broadcasted_iota(jnp.int32, (comps, comps), 0)
    col = lax.broadcasted_iota(jnp.int32, (comps, comps), 1)
    hat = jnp.where(row == col, -2.0, 0.0).astype(F32)
    for step, a in enumerate((own, one, two, three)):
        j = lax.rem(place[0] + PARTS - step, PARTS)
        part = a[rows + 8 : rows + 8 + share, :]
        hat += jnp.where(lax.div(row, share) == j, jnp.concatenate([part] * PARTS, axis=0), 0.0)
    wide = in_ref[0:comps, :]
    sums = in_ref[comps : comps + 8, :]
    loads = (loading_ref[...],) + tuple(a[total : total + comps, :] for a in (far, near, more))
    square = wide[:, 4 * comps : 5 * comps]
    s_hat = mult(sums[:, 4 * comps : 5 * comps], hat)
    for k, out in enumerate(outs):
        here = slice(k * comps, (k + 1) * comps)
        out[0:comps, :] = mult(wide[:, here], hat, ((0,), (0,))) + mult(loads[k], square)
        out[comps : comps + 8, :] = -(mult(s_hat, loads[k], ((1,), (1,))) + sums[:, here])


def deal_body(a_ref, b_ref, c_ref, d_ref, out_ref):
    pieces, _, comps = out_ref.shape
    share = comps // pieces
    total = a_ref[...] + b_ref[...] + c_ref[...] + d_ref[...]
    for p in range(pieces):
        out_ref[p, 0:share, :] = total[p * share : (p + 1) * share, :]
        out_ref[p, share:8, :] = total[comps : comps + 8 - share, :]


def gather_body(pixels, in_ref, out_ref):
    total = jnp.sum(in_ref[...], axis=0) / pixels
    for j in range(out_ref.shape[0]):
        out_ref[j] = total


def last_body(in_ref, load_ref, off_ref):
    pieces = in_ref.shape[0]
    share = load_ref.shape[0] // pieces
    for p in range(pieces):
        load_ref[p * share : (p + 1) * share, :] = in_ref[p, 0:share, :]
    off_ref[...] = in_ref[0, share : share + 1, :]


def on_device(counts, offset, loading):
    pixels = counts.shape[0] * lax.axis_size(WIDE)
    comps = loading.shape[1]
    channels = counts.shape[1] * PARTS * 4
    rows = counts.shape[0] // 4 // PARTS
    share = comps // PARTS
    core = lax.axis_index("c").astype(jnp.int32)
    side = lax.axis_index("zl").astype(jnp.int32)
    place = lax.axis_index("zh").astype(jnp.int32).reshape(1)
    offset = offset.reshape(1, comps)

    swap = [(0, 1), (1, 0)]
    ring = [[(h, (h + k) % PARTS) for h in range(PARTS)] for k in range(PARTS)]
    near_pairs, cross_pairs = [], []
    for z in range(2 * PARTS):
        for c in range(2):
            partner = (((z - c) % (2 * PARTS) ^ 1) + c) % (2 * PARTS)
            near_pairs.append((2 * z + c, 2 * partner + c))
            cross_pairs.append((2 * z + c, 2 * partner + 1 - c))

    near_out = cut(2 * core + 1 - side, counts, loading, offset)
    near = lax.ppermute(near_out, DEEP, near_pairs)
    far_out = cut(2 * (1 - core) + 1 - side, counts, loading, offset)
    far = lax.ppermute(far_out, "c", swap)
    more = lax.ppermute(far, DEEP, near_pairs)
    other = lax.ppermute(cut(2 * (1 - core) + side, counts), "c", swap)
    keep = cut(2 * core + side, counts)
    height = rows + 16 + share
    partial = call(
        encode_body, whole(PARTS, height, comps), keep, other, near, far, loading
    )
    late = (partial, more, loading, offset)
    block = whole(height, comps)
    (two,) = call(functools.partial(encode_last_body, (2,)), (block,), place, *late, scalars=1)
    two = lax.ppermute(two, "zh", ring[2])
    one, three, own = call(
        functools.partial(encode_last_body, (1, 3, 0)), (block,) * 3, place, *late, scalars=1
    )
    one = lax.ppermute(one, "zh", ring[1])
    three = lax.ppermute(three, "zh", ring[3])
    own = call(functools.partial(finish_body, channels), whole(height - 8, comps), own, one, two, three)
    two, one, three = [lax.ppermute(own, "zh", ring[k]) for k in (2, 1, 3)]
    total = whole(comps + 8, 5 * comps)
    common = (place, keep, other, near, far, more, offset)
    grads = call(functools.partial(grad_body, (0,)), total, *common, own, scalars=1)
    grads = call(functools.partial(grad_body, (1, 3)), total, *common, one, three, grads, scalars=1)
    grads = call(functools.partial(grad_body, (2,)), total, *common, two, grads, scalars=1)
    shape = whole(comps + 8, comps)
    mine, to_core, to_near, to_cross = call(
        last_grad_body, (shape,) * 4, place, grads, near, far, more, loading, own, one, two, three, scalars=1
    )
    cross = lax.ppermute(to_cross, DEEP, cross_pairs)
    neared = lax.ppermute(to_near, DEEP, near_pairs)
    cored = lax.ppermute(to_core, "c", swap)
    plane = lax.axis_size(WIDE)
    pieces = call(deal_body, whole(plane, 8, comps), mine, cored, neared, cross)
    pieces = lax.all_to_all(pieces, WIDE, 0, 0)
    pieces = call(functools.partial(gather_body, pixels), whole(plane, 8, comps), pieces)
    pieces = lax.all_to_all(pieces, WIDE, 0, 0)
    grad, grad_offset = call(last_body, (whole(comps, comps), whole(1, comps)), pieces)
    return grad, grad_offset.reshape(comps)


def solution(mesh):
    wide, deep = mesh.devices.shape
    split_mesh = Mesh(mesh.devices.reshape(wide // 4, 4, deep // 4, 2, 2), AXES)
    return jax.shard_map(
        on_device,
        mesh=split_mesh,
        in_specs=(P(WIDE, DEEP), P(DEEP), P(DEEP, None)),
        out_specs=(P(DEEP, None), P(DEEP)),
        check_vma=False,
    )
```

```python
import functools

import jax
import jax.numpy as jnp
from jax import lax
from jax.experimental import pallas as pl
from jax.experimental.pallas import tpu as pltpu
from jax.sharding import Mesh
from jax.sharding import PartitionSpec as P

F32 = jnp.float32
AXES = ("y", "x", "zh", "zl", "c")
WIDE = ("y", "x")
DEEP = ("zh", "zl", "c")
PARTS = 4
LIMIT = 48 * 1024 * 1024
EDGE = 65500000


def mult(left, right, contract=((1,), (0,))):
    return lax.dot_general(
        left, right, (contract, ((), ())),
        preferred_element_type=F32, precision=lax.Precision.HIGHEST,
    )


def whole(*shape):
    return jax.ShapeDtypeStruct(shape, F32)


def call(body, out_shape, *args, scalars=0):
    spaces = [pltpu.SMEM] * scalars + [pltpu.VMEM] * (len(args) - scalars)
    return pl.pallas_call(
        body,
        out_shape=out_shape,
        in_specs=[pl.BlockSpec(memory_space=space) for space in spaces],
        compiler_params=pltpu.CompilerParams(vmem_limit_bytes=LIMIT),
    )(*args)


def cut_body(tail, which, counts_ref, *refs):
    out_ref, held, sem = refs[-3:]
    rows, comps = held.shape
    copy = pltpu.make_async_copy(
        counts_ref.at[pl.ds(pl.multiple_of(which[0] * rows, rows), rows), :], held, sem
    )
    copy.start()
    if tail:
        loading_ref, offset_ref = refs[0:2]
        out_ref[rows : rows + comps, :] = loading_ref[...]
        out_ref[rows + comps : rows + comps + 8, :] = jnp.broadcast_to(offset_ref[...], (8, comps))
    copy.wait()
    out_ref[0:rows, :] = jnp.log(held[...])


def cut(which, counts, tail=()):
    rows, width = counts.shape[0] // 4, counts.shape[1]
    height = rows + (tail[0].shape[0] + 8 if tail else 0)
    return pl.pallas_call(
        functools.partial(cut_body, bool(tail)),
        out_shape=whole(height, width),
        in_specs=[pl.BlockSpec(memory_space=pltpu.SMEM), pl.BlockSpec(memory_space=pl.ANY)]
        + [pl.BlockSpec(memory_space=pltpu.VMEM)] * len(tail),
        scratch_shapes=[pltpu.VMEM((rows, width), F32), pltpu.SemaphoreType.DMA],
        compiler_params=pltpu.CompilerParams(vmem_limit_bytes=EDGE),
    )(which.reshape(1), counts, *tail)


def group_terms(sources, loads, offs):
    both = jnp.concatenate(loads, axis=0)
    bar = jnp.sum(both, axis=0, keepdims=True) / both.shape[0]
    gram = mult(both, both, ((0,), (0,)))
    shift = mult(jnp.concatenate(offs, axis=1), both)
    return bar, both - bar, shift[0:1, :], gram


def log_sums(a, b, at, comps):
    return jnp.sum((a[at : at + comps, :] + b[at : at + comps, :]).T, axis=0, keepdims=True)


def encode_body(keep, near, loading_ref, offset_ref, out_ref):
    total, comps = keep.shape
    rows, share = total // PARTS, comps // PARTS
    bar, bare, shift, gram = group_terms(
        (keep, near),
        (loading_ref[...], near[total : total + comps, :]),
        (jnp.broadcast_to(offset_ref[...], (8, comps)), near[total + comps : total + comps + 8, :]),
    )
    blank = jnp.zeros((1, comps), F32)
    for j in range(PARTS):
        a, b = keep[j * rows : (j + 1) * rows, :], near[j * rows : (j + 1) * rows, :]
        out_ref[j, 0:rows, :] = mult(jnp.concatenate([a, b], axis=1), bare)
        sums = [log_sums(a, b, h * comps, comps) for h in range(2)]
        out_ref[j, rows : rows + 8, :] = jnp.concatenate(
            [sums[0], blank, sums[1], blank, bar, blank, shift, blank], axis=0
        )
        out_ref[j, rows + 8 : rows + 8 + share, :] = gram[j * share : (j + 1) * share, :]


def encode_last_body(in_ref, cross, core, out_ref):
    height, comps = in_ref.shape[1:]
    share = comps // PARTS
    rows = height - 8 - share
    total = PARTS * rows
    bar, bare, shift, gram = group_terms(
        (core, cross),
        [a[total : total + comps, :] for a in (core, cross)],
        [a[total + comps : total + comps + 8, :] for a in (core, cross)],
    )
    blank = jnp.zeros((1, comps), F32)
    for j in range(PARTS):
        a, b = core[j * rows : (j + 1) * rows, :], cross[j * rows : (j + 1) * rows, :]
        out_ref[j, 0:rows, :] = in_ref[j, 0:rows, :] + mult(jnp.concatenate([a, b], axis=1), bare)
        sums = [log_sums(a, b, h * comps, comps) for h in range(2)]
        out_ref[j, rows : rows + 8, :] = in_ref[j, rows : rows + 8, :] + jnp.concatenate(
            [blank, sums[0], blank, sums[1], blank, bar, shift, blank], axis=0
        )
        at = rows + 8
        out_ref[j, at : at + share, :] = in_ref[j, at : at + share, :] + gram[j * share : (j + 1) * share, :]


def finish_body(channels, in_ref, out_ref):
    height, comps = in_ref.shape[1:]
    share = comps // PARTS
    rows = height - 8 - share
    group = channels // (2 * PARTS)
    bars = jnp.concatenate([in_ref[j, rows + 4 : rows + 6, :] for j in range(PARTS)], axis=0)
    shift = sum(in_ref[j, rows + 6 : rows + 7, :] for j in range(PARTS))
    geos = []
    for h in range(2):
        sums = jnp.concatenate(
            [in_ref[j, rows + 2 * h : rows + 2 * h + 2, :] for j in range(PARTS)], axis=0
        )
        geo = jnp.sum(sums, axis=0, keepdims=True) / channels
        at = h * comps
        total = mult(sums - group * geo, bars, ((0,), (0,))) - shift
        for j in range(PARTS):
            total += in_ref[j, at : at + comps, :]
        for j in range(PARTS):
            out_ref[j, at : at + comps, :] = total
        geos.append(geo)
    geos = jnp.concatenate(geos + [jnp.zeros((6, comps), F32)], axis=0)
    gram = sum(in_ref[j, rows + 8 : rows + 8 + share, :] for j in range(PARTS))
    for j in range(PARTS):
        out_ref[j, rows : rows + 8, :] = geos
        out_ref[j, rows + 8 : rows + 8 + share, :] = gram


def grad_body(in_ref, keep, core, near, cross, loading_ref, offset_ref, *outs):
    height, comps = in_ref.shape[1:]
    share = comps // PARTS
    rows = height - 8 - share
    total = PARTS * rows
    gram = jnp.concatenate([in_ref[j, rows + 8 : rows + 8 + share, :] for j in range(PARTS)], axis=0)
    row = lax.broadcasted_iota(jnp.int32, (comps, comps), 0)
    col = lax.broadcasted_iota(jnp.int32, (comps, comps), 1)
    hat = gram - jnp.where(row == col, 2.0, 0.0).astype(F32)
    logs = (keep, core, near, cross)
    loads = (loading_ref[...],) + tuple(a[total : total + comps, :] for a in logs[1:])
    offs = (offset_ref[...],) + tuple(a[total + comps : total + comps + 1, :] for a in logs[1:])
    wide = jnp.zeros((comps, 5 * comps), F32)
    sums = jnp.zeros((1, 5 * comps), F32)
    for j in range(PARTS):
        s = in_ref[j, 0:rows, :]
        geo = jnp.concatenate(
            [
                jnp.broadcast_to(in_ref[j, rows + h : rows + h + 1, :], (comps, comps)).T
                for h in range(2)
            ],
            axis=0,
        )
        both = [a[j * rows : (j + 1) * rows, :] - geo - off for a, off in zip(logs, offs)]
        both = jnp.concatenate(both + [s], axis=1)
        sums += jnp.sum(both, axis=0, keepdims=True)
        wide += mult(s.T, both)
    square = wide[:, 4 * comps : 5 * comps]
    s_hat = mult(jnp.broadcast_to(sums[:, 4 * comps : 5 * comps], (8, comps)), hat)
    for k, out in enumerate(outs):
        here = slice(k * comps, (k + 1) * comps)
        out[0:comps, :] = mult(wide[:, here], hat, ((0,), (0,))) + mult(loads[k], square)
        out[comps : comps + 8, :] = -(mult(s_hat, loads[k], ((1,), (1,))) + sums[:, here])


def deal_body(a_ref, b_ref, c_ref, d_ref, out_ref):
    pieces, _, comps = out_ref.shape
    share = comps // pieces
    total = a_ref[...] + b_ref[...] + c_ref[...] + d_ref[...]
    for p in range(pieces):
        out_ref[p, 0:share, :] = total[p * share : (p + 1) * share, :]
        out_ref[p, share:8, :] = total[comps : comps + 8 - share, :]


def gather_body(pixels, in_ref, out_ref):
    total = jnp.sum(in_ref[...], axis=0) / pixels
    for j in range(out_ref.shape[0]):
        out_ref[j] = total


def last_body(in_ref, load_ref, off_ref):
    pieces = in_ref.shape[0]
    share = load_ref.shape[0] // pieces
    for p in range(pieces):
        load_ref[p * share : (p + 1) * share, :] = in_ref[p, 0:share, :]
    off_ref[...] = in_ref[0, share : share + 1, :]


def on_device(counts, offset, loading):
    pixels = counts.shape[0] * lax.axis_size(WIDE)
    comps = loading.shape[1]
    channels = counts.shape[1] * PARTS * 4
    height = counts.shape[0] // 4 // PARTS + 8 + comps // PARTS
    core = lax.axis_index("c").astype(jnp.int32)
    side = lax.axis_index("zl").astype(jnp.int32)
    offset = offset.reshape(1, comps)

    swap = [(0, 1), (1, 0)]
    near_pairs, cross_pairs = [], []
    for z in range(2 * PARTS):
        for c in range(2):
            partner = (((z - c) % (2 * PARTS) ^ 1) + c) % (2 * PARTS)
            near_pairs.append((2 * z + c, 2 * partner + c))
            cross_pairs.append((2 * z + c, 2 * partner + 1 - c))
    back_pairs = [(b, a) for a, b in cross_pairs]

    tail = (loading, offset)
    near_out = cut(2 * core + 1 - side, counts, tail)
    cross_out = cut(2 * (1 - core) + 1 - side, counts, tail)
    core_out = cut(2 * (1 - core) + side, counts, tail)
    keep = cut(2 * core + side, counts)
    near = lax.ppermute(near_out, DEEP, near_pairs)
    cross = lax.ppermute(cross_out, DEEP, back_pairs)
    other = lax.ppermute(core_out, "c", swap)
    block = whole(PARTS, height, comps)
    partial = call(encode_body, block, keep, near, loading, offset)
    partial = call(encode_last_body, block, partial, cross, other)
    gathered = lax.all_to_all(partial, "zh", 0, 0)
    copies = call(functools.partial(finish_body, channels), block, gathered)
    scores = lax.all_to_all(copies, "zh", 0, 0)
    shape = whole(comps + 8, comps)
    mine, to_core, to_near, to_cross = call(
        grad_body, (shape,) * 4, scores, keep, other, near, cross, loading, offset
    )
    crossed = lax.ppermute(to_cross, DEEP, cross_pairs)
    neared = lax.ppermute(to_near, DEEP, near_pairs)
    cored = lax.ppermute(to_core, "c", swap)
    plane = lax.axis_size(WIDE)
    pieces = call(deal_body, whole(plane, 8, comps), mine, cored, neared, crossed)
    pieces = lax.all_to_all(pieces, WIDE, 0, 0)
    pieces = call(functools.partial(gather_body, pixels), whole(plane, 8, comps), pieces)
    pieces = lax.all_to_all(pieces, WIDE, 0, 0)
    grad, grad_offset = call(last_body, (whole(comps, comps), whole(1, comps)), pieces)
    return grad, grad_offset.reshape(comps)


def solution(mesh):
    wide, deep = mesh.devices.shape
    split_mesh = Mesh(mesh.devices.reshape(wide // 4, 4, deep // 4, 2, 2), AXES)
    return jax.shard_map(
        on_device,
        mesh=split_mesh,
        in_specs=(P(WIDE, DEEP), P(DEEP), P(DEEP, None)),
        out_specs=(P(DEEP, None), P(DEEP)),
        check_vma=False,
    )
```

```python
import functools

import jax
import jax.numpy as jnp
from jax import lax
from jax.experimental import pallas as pl
from jax.experimental.pallas import tpu as pltpu
from jax.sharding import Mesh
from jax.sharding import PartitionSpec as P

F32 = jnp.float32
AXES = ("y", "x", "zh", "zl", "c")
WIDE = ("y", "x")
DEEP = ("zh", "zl", "c")
PARTS = 4
LIMIT = 48 * 1024 * 1024
EDGE = 53500000


def mult(left, right, contract=((1,), (0,))):
    return lax.dot_general(
        left, right, (contract, ((), ())),
        preferred_element_type=F32, precision=lax.Precision.HIGHEST,
    )


def whole(*shape):
    return jax.ShapeDtypeStruct(shape, F32)


def call(body, out_shape, *args, scalars=0):
    spaces = [pltpu.SMEM] * scalars + [pltpu.VMEM] * (len(args) - scalars)
    return pl.pallas_call(
        body,
        out_shape=out_shape,
        in_specs=[pl.BlockSpec(memory_space=space) for space in spaces],
        compiler_params=pltpu.CompilerParams(vmem_limit_bytes=LIMIT),
    )(*args)


def split_body(which, counts_ref, loading_ref, offset_ref, keep, core, near, cross, held, row, sems):
    rows, comps = keep.shape
    outs = (near, cross, core, keep)
    copies = [
        pltpu.make_async_copy(
            counts_ref.at[pl.ds(pl.multiple_of(which[k] * rows, rows), rows), :], held.at[k], sems.at[k]
        )
        for k in range(4)
    ]
    loads = [
        pltpu.make_async_copy(loading_ref, outs[k].at[pl.ds(rows, comps), :], sems.at[4 + k])
        for k in range(3)
    ]
    short = pltpu.make_async_copy(offset_ref, row, sems.at[7])
    for copy in copies + loads + [short]:
        copy.start()
    for k in range(4):
        copies[k].wait()
        outs[k][0:rows, :] = jnp.log(held[k])
    short.wait()
    for k in range(3):
        loads[k].wait()
        outs[k][rows + comps : rows + comps + 8, :] = jnp.broadcast_to(row[...], (8, comps))


def split(which, counts, loading, offset):
    rows, width = counts.shape[0] // 4, counts.shape[1]
    more = rows + loading.shape[0] + 8
    return pl.pallas_call(
        split_body,
        out_shape=(whole(rows, width),) + (whole(more, width),) * 3,
        in_specs=[pl.BlockSpec(memory_space=pltpu.SMEM)] + [pl.BlockSpec(memory_space=pltpu.HBM)] * 3,
        scratch_shapes=[
            pltpu.VMEM((4, rows, width), F32),
            pltpu.VMEM((1, width), F32),
            pltpu.SemaphoreType.DMA((8,)),
        ],
        compiler_params=pltpu.CompilerParams(vmem_limit_bytes=EDGE),
    )(which, counts, loading, offset)


def group_terms(sources, loads, offs):
    both = jnp.concatenate(loads, axis=0)
    bar = jnp.sum(both, axis=0, keepdims=True) / both.shape[0]
    gram = mult(both, both, ((0,), (0,)))
    shift = mult(jnp.concatenate(offs, axis=1), both)
    return bar, both - bar, shift[0:1, :], gram


def log_sums(a, b, at, comps):
    return jnp.sum((a[at : at + comps, :] + b[at : at + comps, :]).T, axis=0, keepdims=True)


def encode_body(keep, near, loading_ref, offset_ref, out_ref):
    total, comps = keep.shape
    rows, share = total // PARTS, comps // PARTS
    bar, bare, shift, gram = group_terms(
        (keep, near),
        (loading_ref[...], near[total : total + comps, :]),
        (jnp.broadcast_to(offset_ref[...], (8, comps)), near[total + comps : total + comps + 8, :]),
    )
    blank = jnp.zeros((1, comps), F32)
    for j in range(PARTS):
        a, b = keep[j * rows : (j + 1) * rows, :], near[j * rows : (j + 1) * rows, :]
        out_ref[j, 0:rows, :] = mult(jnp.concatenate([a, b], axis=1), bare)
        sums = [log_sums(a, b, h * comps, comps) for h in range(2)]
        out_ref[j, rows : rows + 8, :] = jnp.concatenate(
            [sums[0], blank, sums[1], blank, bar, blank, shift, blank], axis=0
        )
        out_ref[j, rows + 8 : rows + 8 + share, :] = gram[j * share : (j + 1) * share, :]


def encode_last_body(in_ref, cross, core, out_ref):
    height, comps = in_ref.shape[1:]
    share = comps // PARTS
    rows = height - 8 - share
    total = PARTS * rows
    bar, bare, shift, gram = group_terms(
        (cross, core),
        [a[total : total + comps, :] for a in (cross, core)],
        [a[total + comps : total + comps + 8, :] for a in (cross, core)],
    )
    blank = jnp.zeros((1, comps), F32)
    for j in range(PARTS):
        a, b = cross[j * rows : (j + 1) * rows, :], core[j * rows : (j + 1) * rows, :]
        out_ref[j, 0:rows, :] = in_ref[j, 0:rows, :] + mult(jnp.concatenate([a, b], axis=1), bare)
        sums = [log_sums(a, b, h * comps, comps) for h in range(2)]
        out_ref[j, rows : rows + 8, :] = in_ref[j, rows : rows + 8, :] + jnp.concatenate(
            [blank, sums[0], blank, sums[1], blank, bar, shift, blank], axis=0
        )
        at = rows + 8
        out_ref[j, at : at + share, :] = in_ref[j, at : at + share, :] + gram[j * share : (j + 1) * share, :]


def finish_body(channels, in_ref, out_ref):
    height, comps = in_ref.shape[1:]
    share = comps // PARTS
    rows = height - 8 - share
    group = channels // (2 * PARTS)
    bars = jnp.concatenate([in_ref[j, rows + 4 : rows + 6, :] for j in range(PARTS)], axis=0)
    shift = sum(in_ref[j, rows + 6 : rows + 7, :] for j in range(PARTS))
    geos = []
    for h in range(2):
        sums = jnp.concatenate(
            [in_ref[j, rows + 2 * h : rows + 2 * h + 2, :] for j in range(PARTS)], axis=0
        )
        geo = jnp.sum(sums, axis=0, keepdims=True) / channels
        at = h * comps
        total = mult(sums - group * geo, bars, ((0,), (0,))) - shift
        for j in range(PARTS):
            total += in_ref[j, at : at + comps, :]
        for j in range(PARTS):
            out_ref[j, at : at + comps, :] = total
        geos.append(geo)
    geos = jnp.concatenate(geos + [jnp.zeros((6, comps), F32)], axis=0)
    gram = sum(in_ref[j, rows + 8 : rows + 8 + share, :] for j in range(PARTS))
    for j in range(PARTS):
        out_ref[j, rows : rows + 8, :] = geos
        out_ref[j, rows + 8 : rows + 8 + share, :] = gram


def grad_body(in_ref, keep, core, near, cross, loading_ref, offset_ref, out_ref):
    height, comps = in_ref.shape[1:]
    share = comps // PARTS
    rows = height - 8 - share
    total = PARTS * rows
    gram = jnp.concatenate([in_ref[j, rows + 8 : rows + 8 + share, :] for j in range(PARTS)], axis=0)
    row = lax.broadcasted_iota(jnp.int32, (comps, comps), 0)
    col = lax.broadcasted_iota(jnp.int32, (comps, comps), 1)
    hat = gram - jnp.where(row == col, 2.0, 0.0).astype(F32)
    logs = (keep, core, near, cross)
    loads = (loading_ref[...],) + tuple(a[total : total + comps, :] for a in logs[1:])
    offs = (offset_ref[...],) + tuple(a[total + comps : total + comps + 1, :] for a in logs[1:])
    wide = jnp.zeros((comps, 5 * comps), F32)
    sums = jnp.zeros((1, 5 * comps), F32)
    for j in range(PARTS):
        s = in_ref[j, 0:rows, :]
        geo = jnp.concatenate(
            [
                jnp.broadcast_to(in_ref[j, rows + h : rows + h + 1, :], (comps, comps)).T
                for h in range(2)
            ],
            axis=0,
        )
        both = [a[j * rows : (j + 1) * rows, :] - geo - off for a, off in zip(logs, offs)]
        both = jnp.concatenate(both + [s], axis=1)
        sums += jnp.sum(both, axis=0, keepdims=True)
        wide += mult(s.T, both)
    square = wide[:, 4 * comps : 5 * comps]
    s_hat = mult(jnp.broadcast_to(sums[:, 4 * comps : 5 * comps], (8, comps)), hat)
    pieces = out_ref.shape[0]
    cut = comps // pieces
    lines = []
    for k in range(4):
        here = slice(k * comps, (k + 1) * comps)
        grad = mult(wide[:, here], hat, ((0,), (0,))) + mult(loads[k], square)
        for p in range(pieces):
            out_ref[p, k * cut : (k + 1) * cut, :] = grad[p * cut : (p + 1) * cut, :]
        lines.append(-(mult(s_hat, loads[k], ((1,), (1,)))[0:1, :] + sums[:, here]))
    lines = jnp.concatenate(lines + lines, axis=0)
    for p in range(pieces):
        out_ref[p, 4 * cut : 4 * cut + 8, :] = lines


def deal_body(in_ref, *outs):
    total = jnp.sum(in_ref[...], axis=0)
    cut = (total.shape[0] - 8) // 4
    for k, out in enumerate(outs):
        line = total[4 * cut + k : 4 * cut + k + 1, :]
        out[...] = jnp.concatenate(
            [total[k * cut : (k + 1) * cut, :], jnp.broadcast_to(line, (8 - cut, line.shape[1]))], axis=0
        )


def gather_body(pixels, a_ref, b_ref, c_ref, d_ref, out_ref):
    total = (a_ref[...] + b_ref[...] + c_ref[...] + d_ref[...]) / pixels
    for j in range(out_ref.shape[0]):
        out_ref[j] = total


def last_body(in_ref, load_ref, off_ref):
    pieces = in_ref.shape[0]
    share = load_ref.shape[0] // pieces
    for p in range(pieces):
        load_ref[p * share : (p + 1) * share, :] = in_ref[p, 0:share, :]
    off_ref[...] = in_ref[0, share : share + 1, :]


def on_device(counts, offset, loading):
    pixels = counts.shape[0] * lax.axis_size(WIDE)
    comps = loading.shape[1]
    channels = counts.shape[1] * PARTS * 4
    height = counts.shape[0] // 4 // PARTS + 8 + comps // PARTS
    core = lax.axis_index("c").astype(jnp.int32)
    side = lax.axis_index("zl").astype(jnp.int32)
    offset = offset.reshape(1, comps)

    swap = [(0, 1), (1, 0)]
    near_pairs, cross_pairs = [], []
    for z in range(2 * PARTS):
        for c in range(2):
            partner = (((z - c) % (2 * PARTS) ^ 1) + c) % (2 * PARTS)
            near_pairs.append((2 * z + c, 2 * partner + c))
            cross_pairs.append((2 * z + c, 2 * partner + 1 - c))
    back_pairs = [(b, a) for a, b in cross_pairs]

    which = jnp.stack(
        [2 * core + 1 - side, 2 * (1 - core) + 1 - side, 2 * (1 - core) + side, 2 * core + side]
    )
    keep, core_out, near_out, cross_out = split(which, counts, loading, offset)
    near = lax.ppermute(near_out, DEEP, near_pairs)
    cross = lax.ppermute(cross_out, DEEP, back_pairs)
    other = lax.ppermute(core_out, "c", swap)
    block = whole(PARTS, height, comps)
    partial = call(encode_body, block, keep, near, loading, offset)
    partial = call(encode_last_body, block, partial, cross, other)
    gathered = lax.all_to_all(partial, "zh", 0, 0)
    copies = call(functools.partial(finish_body, channels), block, gathered)
    scores = lax.all_to_all(copies, "zh", 0, 0)
    plane = lax.axis_size(WIDE)
    pieces = whole(plane, 4 * comps // plane + 8, comps)
    pieces = call(grad_body, pieces, scores, keep, other, near, cross, loading, offset)
    pieces = lax.all_to_all(pieces, WIDE, 0, 0)
    mine, to_core, to_near, to_cross = call(deal_body, (whole(8, comps),) * 4, pieces)
    crossed = lax.ppermute(to_cross, DEEP, cross_pairs)
    neared = lax.ppermute(to_near, DEEP, near_pairs)
    cored = lax.ppermute(to_core, "c", swap)
    pieces = call(
        functools.partial(gather_body, pixels), whole(plane, 8, comps), mine, cored, neared, crossed
    )
    pieces = lax.all_to_all(pieces, WIDE, 0, 0)
    grad, grad_offset = call(last_body, (whole(comps, comps), whole(1, comps)), pieces)
    return grad, grad_offset.reshape(comps)


def solution(mesh):
    wide, deep = mesh.devices.shape
    split_mesh = Mesh(mesh.devices.reshape(wide // 4, 4, deep // 4, 2, 2), AXES)
    return jax.shard_map(
        on_device,
        mesh=split_mesh,
        in_specs=(P(WIDE, DEEP), P(DEEP), P(DEEP, None)),
        out_specs=(P(DEEP, None), P(DEEP)),
        check_vma=False,
    )
```

```python
import functools

import jax
import jax.numpy as jnp
from jax import lax
from jax.experimental import pallas as pl
from jax.experimental.pallas import tpu as pltpu
from jax.sharding import Mesh
from jax.sharding import PartitionSpec as P

F32 = jnp.float32
AXES = ("y", "x", "zh", "zl", "c")
WIDE = ("y", "x")
DEEP = ("zh", "zl", "c")
PARTS = 8
LIMIT = 48 * 1024 * 1024
EDGE = 53500000


def mult(left, right, contract=((1,), (0,))):
    return lax.dot_general(
        left, right, (contract, ((), ())),
        preferred_element_type=F32, precision=lax.Precision.HIGHEST,
    )


def whole(*shape):
    return jax.ShapeDtypeStruct(shape, F32)


def call(body, out_shape, *args, scalars=0):
    spaces = [pltpu.SMEM] * scalars + [pltpu.VMEM] * (len(args) - scalars)
    return pl.pallas_call(
        body,
        out_shape=out_shape,
        in_specs=[pl.BlockSpec(memory_space=space) for space in spaces],
        compiler_params=pltpu.CompilerParams(vmem_limit_bytes=LIMIT),
    )(*args)


def split_body(which, counts_ref, loading_ref, offset_ref, keep, other, held, row, sems):
    rows, comps = keep.shape
    outs = (other, keep)
    copies = [
        pltpu.make_async_copy(
            counts_ref.at[pl.ds(pl.multiple_of(which[k] * rows, rows), rows), :], held.at[k], sems.at[k]
        )
        for k in range(2)
    ]
    copies.append(pltpu.make_async_copy(loading_ref, other.at[pl.ds(rows, comps), :], sems.at[2]))
    copies.append(pltpu.make_async_copy(offset_ref, row, sems.at[3]))
    for copy in copies:
        copy.start()
    for k in range(2):
        copies[k].wait()
        outs[k][0:rows, :] = jnp.log(held[k])
    copies[2].wait()
    copies[3].wait()
    other[rows + comps : rows + comps + 8, :] = jnp.broadcast_to(row[...], (8, comps))


def split(which, counts, loading, offset):
    rows, width = counts.shape[0] // 2, counts.shape[1]
    return pl.pallas_call(
        split_body,
        out_shape=(whole(rows, width), whole(rows + loading.shape[0] + 8, width)),
        in_specs=[pl.BlockSpec(memory_space=pltpu.SMEM)] + [pl.BlockSpec(memory_space=pltpu.HBM)] * 3,
        scratch_shapes=[
            pltpu.VMEM((2, rows, width), F32),
            pltpu.VMEM((1, width), F32),
            pltpu.SemaphoreType.DMA((4,)),
        ],
        compiler_params=pltpu.CompilerParams(vmem_limit_bytes=EDGE),
    )(which, counts, loading, offset)


def encode_body(mine, other, loading_ref, offset_ref, out_ref):
    total, comps = mine.shape
    rows, share = total // PARTS, comps // PARTS
    load = jnp.concatenate([loading_ref[...], other[total : total + comps, :]], axis=0)
    bar = jnp.sum(load, axis=0, keepdims=True) / load.shape[0]
    bare = load - bar
    off = jnp.concatenate(
        [jnp.broadcast_to(offset_ref[...], (8, comps)), other[total + comps : total + comps + 8, :]], axis=1
    )
    shift = mult(off, load)[0:1, :]
    gram = mult(load, load, ((0,), (0,)))
    blank = jnp.zeros((4, comps), F32)
    for j in range(PARTS):
        a, b = mine[j * rows : (j + 1) * rows, :], other[j * rows : (j + 1) * rows, :]
        out_ref[j, 0:rows, :] = mult(jnp.concatenate([a, b], axis=1), bare)
        both = a + b
        sums = [
            jnp.sum(both[h * comps : (h + 1) * comps, :].T, axis=0, keepdims=True) for h in range(2)
        ]
        out_ref[j, rows : rows + 8, :] = jnp.concatenate(sums + [bar, shift, blank], axis=0)
        out_ref[j, rows + 8 : rows + 8 + share, :] = gram[j * share : (j + 1) * share, :]


def finish_body(channels, in_ref, out_ref):
    height, comps = in_ref.shape[1:]
    share = comps // PARTS
    rows = height - 8 - share
    group = channels // PARTS
    bars = jnp.concatenate([in_ref[j, rows + 2 : rows + 3, :] for j in range(PARTS)], axis=0)
    shift = sum(in_ref[j, rows + 3 : rows + 4, :] for j in range(PARTS))
    geos = []
    for h in range(2):
        sums = jnp.concatenate([in_ref[j, rows + h : rows + h + 1, :] for j in range(PARTS)], axis=0)
        geo = jnp.sum(sums, axis=0, keepdims=True) / channels
        at = h * comps
        total = mult(sums - group * geo, bars, ((0,), (0,))) - shift
        for j in range(PARTS):
            total += in_ref[j, at : at + comps, :]
        out_ref[at : at + comps, :] = total
        geos.append(geo)
    out_ref[rows : rows + 8, :] = jnp.concatenate(geos + [jnp.zeros((6, comps), F32)], axis=0)
    out_ref[rows + 8 : rows + 8 + share, :] = sum(in_ref[j, rows + 8 : rows + 8 + share, :] for j in range(PARTS))


def block_terms(first, in_ref, logs, offs):
    blocks, height, comps = in_ref.shape
    rows = height - 8 - comps // PARTS
    wide, sums = 0.0, 0.0
    for j in range(blocks):
        s = in_ref[j, 0:rows, :]
        geo = jnp.concatenate(
            [
                jnp.broadcast_to(in_ref[j, rows + h : rows + h + 1, :], (comps, comps)).T
                for h in range(2)
            ],
            axis=0,
        )
        here = pl.ds(pl.multiple_of((2 * j + first) * rows, rows), rows)
        both = jnp.concatenate([a[here, :] - geo - off for a, off in zip(logs, offs)] + [s], axis=1)
        sums += jnp.sum(both, axis=0, keepdims=True)
        wide += mult(s.T, both)
    return wide, sums


def some_grad_body(side, in_ref, mine, other, offset_ref, out_ref):
    total, comps = mine.shape
    offs = (offset_ref[...], other[total + comps : total + comps + 1, :])
    wide, sums = block_terms(side[0], in_ref, (mine, other), offs)
    out_ref[0:comps, :] = wide
    out_ref[comps : comps + 8, :] = jnp.broadcast_to(sums, (8, sums.shape[1]))


def grad_body(side, near_ref, in_ref, some_ref, mine, other, loading_ref, offset_ref, *outs):
    total, comps = mine.shape
    height = in_ref.shape[1]
    share = comps // PARTS
    rows = height - 8 - share
    offs = (offset_ref[...], other[total + comps : total + comps + 1, :])
    wide, sums = block_terms(1 - side[0], near_ref, (mine, other), offs)
    wide, sums = wide + some_ref[0:comps, :], sums + some_ref[comps : comps + 1, :]
    here = [a[j, rows + 8 : rows + 8 + share, :] for j in range(PARTS // 2) for a in (in_ref, near_ref)]
    there = [a[j, rows + 8 : rows + 8 + share, :] for j in range(PARTS // 2) for a in (near_ref, in_ref)]
    gram = jnp.where(side[0] == 0, jnp.concatenate(here, axis=0), jnp.concatenate(there, axis=0))
    row = lax.broadcasted_iota(jnp.int32, (comps, comps), 0)
    col = lax.broadcasted_iota(jnp.int32, (comps, comps), 1)
    hat = gram - jnp.where(row == col, 2.0, 0.0).astype(F32)
    loads = (loading_ref[...], other[total : total + comps, :])
    square = wide[:, 2 * comps : 3 * comps]
    s_hat = mult(jnp.broadcast_to(sums[:, 2 * comps : 3 * comps], (8, comps)), hat)
    for k, out in enumerate(outs):
        part = slice(k * comps, (k + 1) * comps)
        out[0:comps, :] = mult(wide[:, part], hat, ((0,), (0,))) + mult(loads[k], square)
        out[comps : comps + 8, :] = -(mult(s_hat, loads[k], ((1,), (1,))) + sums[:, part])


def deal_body(a_ref, b_ref, out_ref):
    pieces, _, comps = out_ref.shape
    share = comps // pieces
    total = a_ref[...] + b_ref[...]
    for p in range(pieces):
        out_ref[p, 0:share, :] = total[p * share : (p + 1) * share, :]
        out_ref[p, share:8, :] = total[comps : comps + 8 - share, :]


def gather_body(pixels, in_ref, out_ref):
    total = jnp.sum(in_ref[...], axis=0) / pixels
    for j in range(out_ref.shape[0]):
        out_ref[j] = total


def last_body(in_ref, load_ref, off_ref):
    pieces = in_ref.shape[0]
    share = load_ref.shape[0] // pieces
    for p in range(pieces):
        load_ref[p * share : (p + 1) * share, :] = in_ref[p, 0:share, :]
    off_ref[...] = in_ref[0, share : share + 1, :]


def on_device(counts, offset, loading):
    pixels = counts.shape[0] * lax.axis_size(WIDE)
    comps = loading.shape[1]
    channels = counts.shape[1] * PARTS * 2
    height = counts.shape[0] // 2 // PARTS + 8 + comps // PARTS
    core = lax.axis_index("c").astype(jnp.int32)
    side = lax.axis_index("zl").astype(jnp.int32).reshape(1)
    offset = offset.reshape(1, comps)

    swap = [(0, 1), (1, 0)]
    near_pairs = []
    for z in range(PARTS):
        for c in range(2):
            partner = (((z - c) % PARTS ^ 1) + c) % PARTS
            near_pairs.append((2 * z + c, 2 * partner + c))

    mine, other_out = split(jnp.stack([1 - core, core]), counts, loading, offset)
    other = lax.ppermute(other_out, "c", swap)
    partial = call(encode_body, whole(PARTS, height, comps), mine, other, loading, offset)
    gathered = lax.all_to_all(partial, ("zh", "zl"), 0, 0)
    own = call(functools.partial(finish_body, channels), whole(height, comps), gathered)
    scores = lax.all_gather(own, "zh", axis=0)
    near = lax.ppermute(scores, DEEP, near_pairs)
    some = call(
        some_grad_body, whole(comps + 8, 3 * comps), side, scores, mine, other, offset, scalars=1
    )
    shape = whole(comps + 8, comps)
    grad_mine, grad_other = call(
        grad_body, (shape, shape), side, near, scores, some, mine, other, loading, offset, scalars=1
    )
    arrived = lax.ppermute(grad_other, "c", swap)
    plane = lax.axis_size(WIDE)
    pieces = call(deal_body, whole(plane, 8, comps), grad_mine, arrived)
    pieces = lax.all_to_all(pieces, WIDE, 0, 0)
    pieces = call(functools.partial(gather_body, pixels), whole(plane, 8, comps), pieces)
    pieces = lax.all_to_all(pieces, WIDE, 0, 0)
    grad, grad_offset = call(last_body, (whole(comps, comps), whole(1, comps)), pieces)
    return grad, grad_offset.reshape(comps)


def solution(mesh):
    wide, deep = mesh.devices.shape
    split_mesh = Mesh(mesh.devices.reshape(wide // 4, 4, deep // 4, 2, 2), AXES)
    return jax.shard_map(
        on_device,
        mesh=split_mesh,
        in_specs=(P(WIDE, DEEP), P(DEEP), P(DEEP, None)),
        out_specs=(P(DEEP, None), P(DEEP)),
        check_vma=False,
    )
```

```python
import functools

import jax
import jax.numpy as jnp
from jax import lax
from jax.experimental import pallas as pl
from jax.experimental.pallas import tpu as pltpu
from jax.sharding import Mesh
from jax.sharding import PartitionSpec as P

F32 = jnp.float32
AXES = ("y", "x", "zh", "zl", "c")
WIDE = ("y", "x")
DEEP = ("zh", "zl", "c")
PARTS = 8
LIMIT = 48 * 1024 * 1024


def mult(left, right, contract=((1,), (0,))):
    return lax.dot_general(
        left, right, (contract, ((), ())),
        preferred_element_type=F32, precision=lax.Precision.HIGHEST,
    )


def whole(*shape):
    return jax.ShapeDtypeStruct(shape, F32)


def call(body, out_shape, *args, scalars=0):
    spaces = [pltpu.SMEM] * scalars + [pltpu.VMEM] * (len(args) - scalars)
    return pl.pallas_call(
        body,
        out_shape=out_shape,
        in_specs=[pl.BlockSpec(memory_space=space) for space in spaces],
        compiler_params=pltpu.CompilerParams(vmem_limit_bytes=LIMIT),
    )(*args)


def send_body(which, counts_ref, loading_ref, offset_ref, out_ref, held, row, sems):
    rows, comps = held.shape
    half = rows // 2
    copies = [
        pltpu.make_async_copy(
            counts_ref.at[pl.ds(pl.multiple_of(which[0] * rows + k * half, half), half), :],
            held.at[pl.ds(k * half, half), :],
            sems.at[k],
        )
        for k in range(2)
    ]
    copies.append(pltpu.make_async_copy(loading_ref, out_ref.at[pl.ds(rows, comps), :], sems.at[2]))
    copies.append(pltpu.make_async_copy(offset_ref, row, sems.at[3]))
    for copy in copies:
        copy.start()
    for k in range(2):
        copies[k].wait()
        out_ref[k * half : (k + 1) * half, :] = jnp.log(held[k * half : (k + 1) * half, :])
    copies[2].wait()
    copies[3].wait()
    out_ref[rows + comps : rows + comps + 8, :] = jnp.broadcast_to(row[...], (8, comps))


def keep_body(which, counts_ref, out_ref, held, sem):
    rows = held.shape[0]
    copy = pltpu.make_async_copy(
        counts_ref.at[pl.ds(pl.multiple_of(which[0] * rows, rows), rows), :], held, sem
    )
    copy.start()
    copy.wait()
    out_ref[...] = jnp.log(held[...])


def cut(body, height, scratch, which, counts, *more):
    rows, width = counts.shape[0] // 2, counts.shape[1]
    return pl.pallas_call(
        body,
        out_shape=whole(height, width),
        in_specs=[pl.BlockSpec(memory_space=pltpu.SMEM)]
        + [pl.BlockSpec(memory_space=pltpu.HBM)] * (1 + len(more)),
        scratch_shapes=[pltpu.VMEM((rows, width), F32)] + scratch,
        compiler_params=pltpu.CompilerParams(vmem_limit_bytes=LIMIT),
    )(which.reshape(1), *(pltpu.with_memory_space_constraint(a, pltpu.HBM) for a in (counts,) + more))


def source_terms(load, off):
    bar = jnp.sum(load, axis=0, keepdims=True) / load.shape[0]
    return bar, load - bar, mult(off, load)[0:1, :], mult(load, load, ((0,), (0,)))


def log_sums(logs):
    comps = logs.shape[1]
    return [
        jnp.sum(logs[h * comps : (h + 1) * comps, :].T, axis=0, keepdims=True)
        for h in range(logs.shape[0] // comps)
    ]


def encode_body(mine, loading_ref, offset_ref, out_ref):
    total, comps = mine.shape
    rows, share = total // PARTS, comps // PARTS
    bar, bare, shift, gram = source_terms(
        loading_ref[...], jnp.broadcast_to(offset_ref[...], (8, comps))
    )
    blank = jnp.zeros((1, comps), F32)
    for j in range(PARTS):
        logs = mine[j * rows : (j + 1) * rows, :]
        out_ref[j, 0:rows, :] = mult(logs, bare)
        out_ref[j, rows : rows + 8, :] = jnp.concatenate(
            log_sums(logs) + [blank, blank, bar, blank, shift, blank], axis=0
        )
        out_ref[j, rows + 8 : rows + 8 + share, :] = gram[j * share : (j + 1) * share, :]


def encode_last_body(in_ref, other, out_ref):
    height, comps = in_ref.shape[1:]
    share = comps // PARTS
    rows = height - 8 - share
    total = PARTS * rows
    bar, bare, shift, gram = source_terms(
        other[total : total + comps, :], other[total + comps : total + comps + 8, :]
    )
    blank = jnp.zeros((1, comps), F32)
    for j in range(PARTS):
        logs = other[j * rows : (j + 1) * rows, :]
        out_ref[j, 0:rows, :] = in_ref[j, 0:rows, :] + mult(logs, bare)
        out_ref[j, rows : rows + 8, :] = in_ref[j, rows : rows + 8, :] + jnp.concatenate(
            [blank, blank] + log_sums(logs) + [blank, bar, shift, blank], axis=0
        )
        at = rows + 8
        out_ref[j, at : at + share, :] = in_ref[j, at : at + share, :] + gram[j * share : (j + 1) * share, :]


def finish_body(channels, in_ref, out_ref):
    height, comps = in_ref.shape[1:]
    share = comps // PARTS
    rows = height - 8 - share
    group = channels // (2 * PARTS)
    bars = jnp.concatenate([in_ref[j, rows + 4 : rows + 6, :] for j in range(PARTS)], axis=0)
    shift = sum(in_ref[j, rows + 6 : rows + 7, :] for j in range(PARTS))
    geos = []
    for h in range(2):
        sums = jnp.concatenate(
            [
                in_ref[j, rows + h + k : rows + h + k + 1, :]
                for j in range(PARTS)
                for k in (0, 2)
            ],
            axis=0,
        )
        geo = jnp.sum(sums, axis=0, keepdims=True) / channels
        at = h * comps
        total = mult(sums - group * geo, bars, ((0,), (0,))) - shift
        for j in range(PARTS):
            total += in_ref[j, at : at + comps, :]
        out_ref[at : at + comps, :] = total
        geos.append(geo)
    out_ref[rows : rows + 8, :] = jnp.concatenate(geos + [jnp.zeros((6, comps), F32)], axis=0)
    out_ref[rows + 8 : rows + 8 + share, :] = sum(in_ref[j, rows + 8 : rows + 8 + share, :] for j in range(PARTS))


def block_terms(first, in_ref, logs, offs):
    blocks, height, comps = in_ref.shape
    rows = height - 8 - comps // PARTS
    wide, sums = 0.0, 0.0
    for j in range(blocks):
        s = in_ref[j, 0:rows, :]
        geo = jnp.concatenate(
            [
                jnp.broadcast_to(in_ref[j, rows + h : rows + h + 1, :], (comps, comps)).T
                for h in range(2)
            ],
            axis=0,
        )
        here = pl.ds(pl.multiple_of((2 * j + first) * rows, rows), rows)
        both = jnp.concatenate([a[here, :] - geo - off for a, off in zip(logs, offs)] + [s], axis=1)
        sums += jnp.sum(both, axis=0, keepdims=True)
        wide += mult(s.T, both)
    return wide, sums


def some_grad_body(side, in_ref, mine, other, offset_ref, out_ref):
    total, comps = mine.shape
    offs = (offset_ref[...], other[total + comps : total + comps + 1, :])
    wide, sums = block_terms(side[0], in_ref, (mine, other), offs)
    out_ref[0:comps, :] = wide
    out_ref[comps : comps + 8, :] = jnp.broadcast_to(sums, (8, sums.shape[1]))


def grad_body(side, near_ref, in_ref, some_ref, mine, other, offset_ref, out_ref, rest_ref):
    total, comps = mine.shape
    height = in_ref.shape[1]
    share = comps // PARTS
    rows = height - 8 - share
    offs = (offset_ref[...], other[total + comps : total + comps + 1, :])
    wide, sums = block_terms(1 - side[0], near_ref, (mine, other), offs)
    wide, sums = wide + some_ref[0:comps, :], sums + some_ref[comps : comps + 1, :]
    here = [a[j, rows + 8 : rows + 8 + share, :] for j in range(PARTS // 2) for a in (in_ref, near_ref)]
    there = [a[j, rows + 8 : rows + 8 + share, :] for j in range(PARTS // 2) for a in (near_ref, in_ref)]
    gram = jnp.where(side[0] == 0, jnp.concatenate(here, axis=0), jnp.concatenate(there, axis=0))
    row = lax.broadcasted_iota(jnp.int32, (comps, comps), 0)
    col = lax.broadcasted_iota(jnp.int32, (comps, comps), 1)
    hat = gram - jnp.where(row == col, 2.0, 0.0).astype(F32)
    square = wide[:, 2 * comps : 3 * comps]
    s_sum, c_mine, c_other = (sums[:, k * comps : (k + 1) * comps] for k in (2, 0, 1))
    source_grad(wide[:, comps : 2 * comps], hat, square, s_sum, c_other, other[total : total + comps, :], out_ref)
    rest_ref[0] = wide[:, 0:comps]
    rest_ref[1] = hat
    rest_ref[2] = square
    rest_ref[3] = jnp.broadcast_to(s_sum, (comps, comps))
    rest_ref[4] = jnp.broadcast_to(c_mine, (comps, comps))


def source_grad(w_turned, hat, square, s_sum, c_sum, load, out_ref):
    comps = load.shape[1]
    s_hat = mult(jnp.broadcast_to(s_sum, (8, comps)), hat)
    out_ref[0:comps, :] = mult(w_turned, hat, ((0,), (0,))) + mult(load, square)
    out_ref[comps : comps + 8, :] = -(mult(s_hat, load, ((1,), (1,))) + c_sum)


def mine_grad_body(rest_ref, loading_ref, out_ref):
    source_grad(
        rest_ref[0], rest_ref[1], rest_ref[2], rest_ref[3, 0:1, :], rest_ref[4, 0:1, :], loading_ref[...], out_ref
    )


def deal_body(a_ref, b_ref, out_ref):
    pieces, _, comps = out_ref.shape
    share = comps // pieces
    total = a_ref[...] + b_ref[...]
    for p in range(pieces):
        out_ref[p, 0:share, :] = total[p * share : (p + 1) * share, :]
        out_ref[p, share:8, :] = total[comps : comps + 8 - share, :]


def gather_body(pixels, in_ref, out_ref):
    total = jnp.sum(in_ref[...], axis=0) / pixels
    for j in range(out_ref.shape[0]):
        out_ref[j] = total


def last_body(in_ref, load_ref, off_ref):
    pieces = in_ref.shape[0]
    share = load_ref.shape[0] // pieces
    for p in range(pieces):
        load_ref[p * share : (p + 1) * share, :] = in_ref[p, 0:share, :]
    off_ref[...] = in_ref[0, share : share + 1, :]


def on_device(counts, offset, loading):
    pixels = counts.shape[0] * lax.axis_size(WIDE)
    comps = loading.shape[1]
    channels = counts.shape[1] * PARTS * 2
    height = counts.shape[0] // 2 // PARTS + 8 + comps // PARTS
    core = lax.axis_index("c").astype(jnp.int32)
    side = lax.axis_index("zl").astype(jnp.int32).reshape(1)
    offset = offset.reshape(1, comps)

    swap = [(0, 1), (1, 0)]
    near_pairs = []
    for z in range(PARTS):
        for c in range(2):
            partner = (((z - c) % PARTS ^ 1) + c) % PARTS
            near_pairs.append((2 * z + c, 2 * partner + c))

    half = counts.shape[0] // 2
    scratch = [pltpu.VMEM((1, comps), F32), pltpu.SemaphoreType.DMA((4,))]
    sent = cut(send_body, half + comps + 8, scratch, 1 - core, counts, loading, offset)
    other = lax.ppermute(sent, "c", swap)
    mine = cut(keep_body, half, [pltpu.SemaphoreType.DMA], core, counts)
    block = whole(PARTS, height, comps)
    partial = call(encode_body, block, mine, loading, offset)
    partial = call(encode_last_body, block, partial, other)
    gathered = lax.all_to_all(partial, ("zh", "zl"), 0, 0)
    own = call(functools.partial(finish_body, channels), whole(height, comps), gathered)
    scores = lax.all_gather(own, "zh", axis=0)
    near = lax.ppermute(scores, DEEP, near_pairs)
    some = call(
        some_grad_body, whole(comps + 8, 3 * comps), side, scores, mine, other, offset, scalars=1
    )
    shape = whole(comps + 8, comps)
    grad_other, rest = call(
        grad_body, (shape, whole(5, comps, comps)), side, near, scores, some, mine, other, offset, scalars=1
    )
    arrived = lax.ppermute(grad_other, "c", swap)
    grad_mine = call(mine_grad_body, shape, rest, loading)
    plane = lax.axis_size(WIDE)
    pieces = call(deal_body, whole(plane, 8, comps), grad_mine, arrived)
    pieces = lax.all_to_all(pieces, WIDE, 0, 0)
    pieces = call(functools.partial(gather_body, pixels), whole(plane, 8, comps), pieces)
    pieces = lax.all_to_all(pieces, WIDE, 0, 0)
    grad, grad_offset = call(last_body, (whole(comps, comps), whole(1, comps)), pieces)
    return grad, grad_offset.reshape(comps)


def solution(mesh):
    wide, deep = mesh.devices.shape
    split_mesh = Mesh(mesh.devices.reshape(wide // 4, 4, deep // 4, 2, 2), AXES)
    return jax.shard_map(
        on_device,
        mesh=split_mesh,
        in_specs=(P(WIDE, DEEP), P(DEEP), P(DEEP, None)),
        out_specs=(P(DEEP, None), P(DEEP)),
        check_vma=False,
    )
```

```python
import functools

import jax
import jax.numpy as jnp
from jax import lax
from jax.experimental import pallas as pl
from jax.experimental.pallas import tpu as pltpu
from jax.sharding import Mesh
from jax.sharding import PartitionSpec as P

F32 = jnp.float32
AXES = ("y", "x", "zh", "zl", "c")
WIDE = ("y", "x")
DEEP = ("zh", "zl", "c")
PARTS = 8
LIMIT = 48 * 1024 * 1024


def mult(left, right, contract=((1,), (0,))):
    return lax.dot_general(
        left, right, (contract, ((), ())),
        preferred_element_type=F32, precision=lax.Precision.HIGHEST,
    )


def whole(*shape):
    return jax.ShapeDtypeStruct(shape, F32)


def call(body, out_shape, *args, scalars=0):
    spaces = [pltpu.SMEM] * scalars + [pltpu.VMEM] * (len(args) - scalars)
    return pl.pallas_call(
        body,
        out_shape=out_shape,
        in_specs=[pl.BlockSpec(memory_space=space) for space in spaces],
        compiler_params=pltpu.CompilerParams(vmem_limit_bytes=LIMIT),
    )(*args)


def send_body(which, counts_ref, loading_ref, offset_ref, out_ref, held, row, sems):
    rows, comps = held.shape
    half = rows // 2
    copies = [
        pltpu.make_async_copy(
            counts_ref.at[pl.ds(pl.multiple_of(which[0] * rows + k * half, half), half), :],
            held.at[pl.ds(k * half, half), :],
            sems.at[k],
        )
        for k in range(2)
    ]
    copies.append(pltpu.make_async_copy(loading_ref, out_ref.at[pl.ds(rows, comps), :], sems.at[2]))
    copies.append(pltpu.make_async_copy(offset_ref, row, sems.at[3]))
    for copy in copies:
        copy.start()
    for k in range(2):
        copies[k].wait()
        out_ref[k * half : (k + 1) * half, :] = jnp.log(held[k * half : (k + 1) * half, :])
    copies[2].wait()
    copies[3].wait()
    out_ref[rows + comps : rows + comps + 8, :] = jnp.broadcast_to(row[...], (8, comps))


def keep_body(which, counts_ref, out_ref, held, sem):
    rows = held.shape[0]
    copy = pltpu.make_async_copy(
        counts_ref.at[pl.ds(pl.multiple_of(which[0] * rows, rows), rows), :], held, sem
    )
    copy.start()
    copy.wait()
    out_ref[...] = jnp.log(held[...])


def cut(body, height, scratch, which, counts, *more):
    rows, width = counts.shape[0] // 2, counts.shape[1]
    return pl.pallas_call(
        body,
        out_shape=whole(height, width),
        in_specs=[pl.BlockSpec(memory_space=pltpu.SMEM)]
        + [pl.BlockSpec(memory_space=pltpu.HBM)] * (1 + len(more)),
        scratch_shapes=[pltpu.VMEM((rows, width), F32)] + scratch,
        compiler_params=pltpu.CompilerParams(vmem_limit_bytes=LIMIT),
    )(which.reshape(1), *(pltpu.with_memory_space_constraint(a, pltpu.HBM) for a in (counts,) + more))


def source_terms(load, off):
    bar = jnp.sum(load, axis=0, keepdims=True) / load.shape[0]
    return bar, load - bar, mult(off, load)[0:1, :], mult(load, load, ((0,), (0,)))


def log_sums(logs):
    comps = logs.shape[1]
    return [
        jnp.sum(logs[h * comps : (h + 1) * comps, :].T, axis=0, keepdims=True)
        for h in range(logs.shape[0] // comps)
    ]


def encode_body(mine, loading_ref, offset_ref, out_ref):
    total, comps = mine.shape
    rows, share = total // PARTS, comps // PARTS
    bar, bare, shift, gram = source_terms(
        loading_ref[...], jnp.broadcast_to(offset_ref[...], (8, comps))
    )
    blank = jnp.zeros((1, comps), F32)
    for j in range(PARTS):
        logs = mine[j * rows : (j + 1) * rows, :]
        out_ref[j, 0:rows, :] = mult(logs, bare)
        out_ref[j, rows : rows + 8, :] = jnp.concatenate(
            log_sums(logs) + [blank, blank, bar, blank, shift, blank], axis=0
        )
        out_ref[j, rows + 8 : rows + 8 + share, :] = gram[j * share : (j + 1) * share, :]


def encode_last_body(in_ref, other, out_ref):
    height, comps = in_ref.shape[1:]
    share = comps // PARTS
    rows = height - 8 - share
    total = PARTS * rows
    bar, bare, shift, gram = source_terms(
        other[total : total + comps, :], other[total + comps : total + comps + 8, :]
    )
    blank = jnp.zeros((1, comps), F32)
    for j in range(PARTS):
        logs = other[j * rows : (j + 1) * rows, :]
        out_ref[j, 0:rows, :] = in_ref[j, 0:rows, :] + mult(logs, bare)
        out_ref[j, rows : rows + 8, :] = in_ref[j, rows : rows + 8, :] + jnp.concatenate(
            [blank, blank] + log_sums(logs) + [blank, bar, shift, blank], axis=0
        )
        at = rows + 8
        out_ref[j, at : at + share, :] = in_ref[j, at : at + share, :] + gram[j * share : (j + 1) * share, :]


def finish_body(channels, in_ref, out_ref):
    height, comps = in_ref.shape[1:]
    share = comps // PARTS
    rows = height - 8 - share
    group = channels // (2 * PARTS)
    bars = jnp.concatenate([in_ref[j, rows + 4 : rows + 6, :] for j in range(PARTS)], axis=0)
    shift = sum(in_ref[j, rows + 6 : rows + 7, :] for j in range(PARTS))
    geos = []
    for h in range(2):
        sums = jnp.concatenate(
            [
                in_ref[j, rows + h + k : rows + h + k + 1, :]
                for j in range(PARTS)
                for k in (0, 2)
            ],
            axis=0,
        )
        geo = jnp.sum(sums, axis=0, keepdims=True) / channels
        at = h * comps
        total = mult(sums - group * geo, bars, ((0,), (0,))) - shift
        for j in range(PARTS):
            total += in_ref[j, at : at + comps, :]
        out_ref[at : at + comps, :] = total
        geos.append(geo)
    out_ref[rows : rows + 8, :] = jnp.concatenate(geos + [jnp.zeros((6, comps), F32)], axis=0)
    out_ref[rows + 8 : rows + 8 + share, :] = sum(in_ref[j, rows + 8 : rows + 8 + share, :] for j in range(PARTS))


def block_terms(first, in_ref, logs, offs):
    blocks, height, comps = in_ref.shape
    rows = height - 8 - comps // PARTS
    wide, sums = 0.0, 0.0
    for j in range(blocks):
        s = in_ref[j, 0:rows, :]
        geo = jnp.concatenate(
            [
                jnp.broadcast_to(in_ref[j, rows + h : rows + h + 1, :], (comps, comps)).T
                for h in range(2)
            ],
            axis=0,
        )
        here = pl.ds(pl.multiple_of((2 * j + first) * rows, rows), rows)
        both = jnp.concatenate([a[here, :] - geo - off for a, off in zip(logs, offs)] + [s], axis=1)
        sums += jnp.sum(both, axis=0, keepdims=True)
        wide += mult(s.T, both)
    return wide, sums


def some_grad_body(side, in_ref, mine, other, offset_ref, out_ref):
    total, comps = mine.shape
    offs = (offset_ref[...], other[total + comps : total + comps + 1, :])
    wide, sums = block_terms(side[0], in_ref, (mine, other), offs)
    out_ref[0:comps, :] = wide
    out_ref[comps : comps + 8, :] = jnp.broadcast_to(sums, (8, sums.shape[1]))


def grad_body(side, near_ref, in_ref, some_ref, mine, other, offset_ref, out_ref, rest_ref):
    total, comps = mine.shape
    height = in_ref.shape[1]
    share = comps // PARTS
    rows = height - 8 - share
    offs = (offset_ref[...], other[total + comps : total + comps + 1, :])
    wide, sums = block_terms(1 - side[0], near_ref, (mine, other), offs)
    wide, sums = wide + some_ref[0:comps, :], sums + some_ref[comps : comps + 1, :]
    here = [a[j, rows + 8 : rows + 8 + share, :] for j in range(PARTS // 2) for a in (in_ref, near_ref)]
    there = [a[j, rows + 8 : rows + 8 + share, :] for j in range(PARTS // 2) for a in (near_ref, in_ref)]
    gram = jnp.where(side[0] == 0, jnp.concatenate(here, axis=0), jnp.concatenate(there, axis=0))
    row = lax.broadcasted_iota(jnp.int32, (comps, comps), 0)
    col = lax.broadcasted_iota(jnp.int32, (comps, comps), 1)
    hat = gram - jnp.where(row == col, 2.0, 0.0).astype(F32)
    square = wide[:, 2 * comps : 3 * comps]
    s_sum, c_mine, c_other = (sums[:, k * comps : (k + 1) * comps] for k in (2, 0, 1))
    source_grad(wide[:, comps : 2 * comps], hat, square, s_sum, c_other, other[total : total + comps, :], out_ref)
    rest_ref[0] = wide[:, 0:comps]
    rest_ref[1] = hat
    rest_ref[2] = square
    rest_ref[3] = jnp.broadcast_to(s_sum, (comps, comps))
    rest_ref[4] = jnp.broadcast_to(c_mine, (comps, comps))


def source_grad(w_turned, hat, square, s_sum, c_sum, load, out_ref):
    comps = load.shape[1]
    s_hat = mult(jnp.broadcast_to(s_sum, (8, comps)), hat)
    out_ref[0:comps, :] = mult(w_turned, hat, ((0,), (0,))) + mult(load, square)
    out_ref[comps : comps + 8, :] = -(mult(s_hat, load, ((1,), (1,))) + c_sum)


def mine_grad_body(rest_ref, loading_ref, out_ref):
    source_grad(
        rest_ref[0], rest_ref[1], rest_ref[2], rest_ref[3, 0:1, :], rest_ref[4, 0:1, :], loading_ref[...], out_ref
    )


def deal_body(a_ref, b_ref, out_ref):
    pieces, _, comps = out_ref.shape
    share = comps // pieces
    total = a_ref[...] + b_ref[...]
    for p in range(pieces):
        out_ref[p, 0:share, :] = total[p * share : (p + 1) * share, :]
        out_ref[p, share:8, :] = total[comps : comps + 8 - share, :]


def gather_body(pixels, in_ref, out_ref):
    total = jnp.sum(in_ref[...], axis=0) / pixels
    for j in range(out_ref.shape[0]):
        out_ref[j] = total


def last_body(in_ref, load_ref, off_ref):
    pieces = in_ref.shape[0]
    share = load_ref.shape[0] // pieces
    for p in range(pieces):
        load_ref[p * share : (p + 1) * share, :] = in_ref[p, 0:share, :]
    off_ref[...] = in_ref[0, share : share + 1, :]


def on_device(counts, offset, loading):
    pixels = counts.shape[0] * lax.axis_size(WIDE)
    comps = loading.shape[1]
    channels = counts.shape[1] * PARTS * 2
    height = counts.shape[0] // 2 // PARTS + 8 + comps // PARTS
    core = lax.axis_index("c").astype(jnp.int32)
    side = (lax.axis_index("zl") ^ lax.axis_index("c")).astype(jnp.int32).reshape(1)
    offset = offset.reshape(1, comps)

    swap = [(0, 1), (1, 0)]
    near_pairs = []
    for z in range(PARTS):
        for c in range(2):
            partner = (((z - c) % PARTS ^ 1) + c) % PARTS
            near_pairs.append((2 * z + c, 2 * partner + c))

    rings = [[2 * z for z in range(PARTS)], [2 * z + 1 for z in reversed(range(PARTS))]]
    rings4 = [ring[k::2] for ring in rings for k in range(2)]
    plane = lax.axis_size(WIDE)
    planes = [
        [2 * (PARTS * p + z) + c for p in (reversed(range(plane)) if c else range(plane))]
        for z in range(PARTS)
        for c in range(2)
    ]

    half = counts.shape[0] // 2
    scratch = [pltpu.VMEM((1, comps), F32), pltpu.SemaphoreType.DMA((4,))]
    sent = cut(send_body, half + comps + 8, scratch, 1 - core, counts, loading, offset)
    other = lax.ppermute(sent, "c", swap)
    mine = cut(keep_body, half, [pltpu.SemaphoreType.DMA], core, counts)
    block = whole(PARTS, height, comps)
    partial = call(encode_body, block, mine, loading, offset)
    partial = call(encode_last_body, block, partial, other)
    gathered = lax.all_to_all(partial, DEEP, 0, 0, axis_index_groups=rings)
    own = call(functools.partial(finish_body, channels), whole(height, comps), gathered)
    scores = lax.all_gather(own, DEEP, axis=0, axis_index_groups=rings4)
    near = lax.ppermute(scores, DEEP, near_pairs)
    some = call(
        some_grad_body, whole(comps + 8, 3 * comps), side, scores, mine, other, offset, scalars=1
    )
    shape = whole(comps + 8, comps)
    grad_other, rest = call(
        grad_body, (shape, whole(5, comps, comps)), side, near, scores, some, mine, other, offset, scalars=1
    )
    arrived = lax.ppermute(grad_other, "c", swap)
    grad_mine = call(mine_grad_body, shape, rest, loading)
    pieces = call(deal_body, whole(plane, 8, comps), grad_mine, arrived)
    pieces = lax.all_to_all(pieces, AXES, 0, 0, axis_index_groups=planes)
    pieces = call(functools.partial(gather_body, pixels), whole(plane, 8, comps), pieces)
    pieces = lax.all_to_all(pieces, AXES, 0, 0, axis_index_groups=planes)
    grad, grad_offset = call(last_body, (whole(comps, comps), whole(1, comps)), pieces)
    return grad, grad_offset.reshape(comps)


def solution(mesh):
    wide, deep = mesh.devices.shape
    split_mesh = Mesh(mesh.devices.reshape(wide // 4, 4, deep // 4, 2, 2), AXES)
    return jax.shard_map(
        on_device,
        mesh=split_mesh,
        in_specs=(P(WIDE, DEEP), P(DEEP), P(DEEP, None)),
        out_specs=(P(DEEP, None), P(DEEP)),
        check_vma=False,
    )
```

```python
import functools

import jax
import jax.numpy as jnp
from jax import lax
from jax.experimental import pallas as pl
from jax.experimental.pallas import tpu as pltpu
from jax.sharding import Mesh
from jax.sharding import PartitionSpec as P

F32 = jnp.float32
AXES = ("y", "x", "zh", "zl", "c")
WIDE = ("y", "x")
DEEP = ("zh", "zl", "c")
PARTS = 8
LIMIT = 48 * 1024 * 1024


def mult(left, right, contract=((1,), (0,))):
    return lax.dot_general(
        left, right, (contract, ((), ())),
        preferred_element_type=F32, precision=lax.Precision.HIGHEST,
    )


def whole(*shape):
    return jax.ShapeDtypeStruct(shape, F32)


def call(body, out_shape, *args, scalars=0):
    spaces = [pltpu.SMEM] * scalars + [pltpu.VMEM] * (len(args) - scalars)
    return pl.pallas_call(
        body,
        out_shape=out_shape,
        in_specs=[pl.BlockSpec(memory_space=space) for space in spaces],
        compiler_params=pltpu.CompilerParams(vmem_limit_bytes=LIMIT),
    )(*args)


def send_body(which, counts_ref, loading_ref, offset_ref, out_ref, held, row, sems):
    rows, comps = held.shape
    half = rows // 2
    copies = [
        pltpu.make_async_copy(
            counts_ref.at[pl.ds(pl.multiple_of(which[0] * rows + k * half, half), half), :],
            held.at[pl.ds(k * half, half), :],
            sems.at[k],
        )
        for k in range(2)
    ]
    copies.append(pltpu.make_async_copy(loading_ref, out_ref.at[pl.ds(rows, comps), :], sems.at[2]))
    copies.append(pltpu.make_async_copy(offset_ref, row, sems.at[3]))
    for copy in copies:
        copy.start()
    for k in range(2):
        copies[k].wait()
        out_ref[k * half : (k + 1) * half, :] = jnp.log(held[k * half : (k + 1) * half, :])
    copies[2].wait()
    copies[3].wait()
    out_ref[rows + comps : rows + comps + 8, :] = jnp.broadcast_to(row[...], (8, comps))


def keep_body(which, counts_ref, out_ref, held, sem):
    rows = held.shape[0]
    copy = pltpu.make_async_copy(
        counts_ref.at[pl.ds(pl.multiple_of(which[0] * rows, rows), rows), :], held, sem
    )
    copy.start()
    copy.wait()
    out_ref[...] = jnp.log(held[...])


def cut(body, height, scratch, which, counts, *more):
    rows, width = counts.shape[0] // 2, counts.shape[1]
    return pl.pallas_call(
        body,
        out_shape=whole(height, width),
        in_specs=[pl.BlockSpec(memory_space=pltpu.SMEM)]
        + [pl.BlockSpec(memory_space=pltpu.HBM)] * (1 + len(more)),
        scratch_shapes=[pltpu.VMEM((rows, width), F32)] + scratch,
        compiler_params=pltpu.CompilerParams(vmem_limit_bytes=LIMIT),
    )(which.reshape(1), *(pltpu.with_memory_space_constraint(a, pltpu.HBM) for a in (counts,) + more))


def source_terms(load, off):
    bar = jnp.sum(load, axis=0, keepdims=True) / load.shape[0]
    return bar, load - bar, mult(off, load)[0:1, :], mult(load, load, ((0,), (0,)))


def log_sums(logs):
    comps = logs.shape[1]
    return [
        jnp.sum(logs[h * comps : (h + 1) * comps, :].T, axis=0, keepdims=True)
        for h in range(logs.shape[0] // comps)
    ]


def encode_body(mine, loading_ref, offset_ref, out_ref):
    total, comps = mine.shape
    rows, share = total // PARTS, comps // PARTS
    bar, bare, shift, gram = source_terms(
        loading_ref[...], jnp.broadcast_to(offset_ref[...], (8, comps))
    )
    blank = jnp.zeros((1, comps), F32)
    for j in range(PARTS):
        logs = mine[j * rows : (j + 1) * rows, :]
        out_ref[j, 0:rows, :] = mult(logs, bare)
        out_ref[j, rows : rows + 8, :] = jnp.concatenate(
            log_sums(logs) + [blank, blank, bar, blank, shift, blank], axis=0
        )
        out_ref[j, rows + 8 : rows + 8 + share, :] = gram[j * share : (j + 1) * share, :]


def encode_last_body(in_ref, other, out_ref):
    height, comps = in_ref.shape[1:]
    share = comps // PARTS
    rows = height - 8 - share
    total = PARTS * rows
    bar, bare, shift, gram = source_terms(
        other[total : total + comps, :], other[total + comps : total + comps + 8, :]
    )
    blank = jnp.zeros((1, comps), F32)
    for j in range(PARTS):
        logs = other[j * rows : (j + 1) * rows, :]
        out_ref[j, 0:rows, :] = in_ref[j, 0:rows, :] + mult(logs, bare)
        out_ref[j, rows : rows + 8, :] = in_ref[j, rows : rows + 8, :] + jnp.concatenate(
            [blank, blank] + log_sums(logs) + [blank, bar, shift, blank], axis=0
        )
        at = rows + 8
        out_ref[j, at : at + share, :] = in_ref[j, at : at + share, :] + gram[j * share : (j + 1) * share, :]


def finish_body(channels, in_ref, out_ref):
    height, comps = in_ref.shape[1:]
    share = comps // PARTS
    rows = height - 8 - share
    group = channels // (2 * PARTS)
    bars = jnp.concatenate([in_ref[j, rows + 4 : rows + 6, :] for j in range(PARTS)], axis=0)
    shift = sum(in_ref[j, rows + 6 : rows + 7, :] for j in range(PARTS))
    geos = []
    for h in range(2):
        sums = jnp.concatenate(
            [
                in_ref[j, rows + h + k : rows + h + k + 1, :]
                for j in range(PARTS)
                for k in (0, 2)
            ],
            axis=0,
        )
        geo = jnp.sum(sums, axis=0, keepdims=True) / channels
        at = h * comps
        total = mult(sums - group * geo, bars, ((0,), (0,))) - shift
        for j in range(PARTS):
            total += in_ref[j, at : at + comps, :]
        out_ref[at : at + comps, :] = total
        geos.append(geo)
    out_ref[rows : rows + 8, :] = jnp.concatenate(geos + [jnp.zeros((6, comps), F32)], axis=0)
    out_ref[rows + 8 : rows + 8 + share, :] = sum(in_ref[j, rows + 8 : rows + 8 + share, :] for j in range(PARTS))


def block_terms(first, in_ref, logs, offs):
    blocks, height, comps = in_ref.shape
    rows = height - 8 - comps // PARTS
    wide, sums = 0.0, 0.0
    for j in range(blocks):
        s = in_ref[j, 0:rows, :]
        geo = jnp.concatenate(
            [
                jnp.broadcast_to(in_ref[j, rows + h : rows + h + 1, :], (comps, comps)).T
                for h in range(2)
            ],
            axis=0,
        )
        here = pl.ds(pl.multiple_of((2 * j + first) * rows, rows), rows)
        both = jnp.concatenate([a[here, :] - geo - off for a, off in zip(logs, offs)] + [s], axis=1)
        sums += jnp.sum(both, axis=0, keepdims=True)
        wide += mult(s.T, both)
    return wide, sums


def some_grad_body(side, in_ref, mine, other, offset_ref, out_ref):
    total, comps = mine.shape
    offs = (offset_ref[...], other[total + comps : total + comps + 1, :])
    wide, sums = block_terms(side[0], in_ref, (mine, other), offs)
    out_ref[0:comps, :] = wide
    out_ref[comps : comps + 8, :] = jnp.broadcast_to(sums, (8, sums.shape[1]))


def grad_body(side, near_ref, in_ref, some_ref, mine, other, offset_ref, out_ref, rest_ref):
    total, comps = mine.shape
    height = in_ref.shape[1]
    share = comps // PARTS
    rows = height - 8 - share
    offs = (offset_ref[...], other[total + comps : total + comps + 1, :])
    wide, sums = block_terms(1 - side[0], near_ref, (mine, other), offs)
    wide, sums = wide + some_ref[0:comps, :], sums + some_ref[comps : comps + 1, :]
    here = [a[j, rows + 8 : rows + 8 + share, :] for j in range(PARTS // 2) for a in (in_ref, near_ref)]
    there = [a[j, rows + 8 : rows + 8 + share, :] for j in range(PARTS // 2) for a in (near_ref, in_ref)]
    gram = jnp.where(side[0] == 0, jnp.concatenate(here, axis=0), jnp.concatenate(there, axis=0))
    row = lax.broadcasted_iota(jnp.int32, (comps, comps), 0)
    col = lax.broadcasted_iota(jnp.int32, (comps, comps), 1)
    hat = gram - jnp.where(row == col, 2.0, 0.0).astype(F32)
    square = wide[:, 2 * comps : 3 * comps]
    s_sum, c_mine, c_other = (sums[:, k * comps : (k + 1) * comps] for k in (2, 0, 1))
    source_grad(wide[:, comps : 2 * comps], hat, square, s_sum, c_other, other[total : total + comps, :], out_ref)
    rest_ref[0] = wide[:, 0:comps]
    rest_ref[1] = hat
    rest_ref[2] = square
    rest_ref[3] = jnp.broadcast_to(s_sum, (comps, comps))
    rest_ref[4] = jnp.broadcast_to(c_mine, (comps, comps))


def source_grad(w_turned, hat, square, s_sum, c_sum, load, out_ref):
    comps = load.shape[1]
    s_hat = mult(jnp.broadcast_to(s_sum, (8, comps)), hat)
    out_ref[0:comps, :] = mult(w_turned, hat, ((0,), (0,))) + mult(load, square)
    out_ref[comps : comps + 8, :] = -(mult(s_hat, load, ((1,), (1,))) + c_sum)


def mine_grad_body(rest_ref, loading_ref, out_ref):
    source_grad(
        rest_ref[0], rest_ref[1], rest_ref[2], rest_ref[3, 0:1, :], rest_ref[4, 0:1, :], loading_ref[...], out_ref
    )


def deal_body(a_ref, b_ref, out_ref):
    pieces, _, comps = out_ref.shape
    share = comps // pieces
    total = a_ref[...] + b_ref[...]
    for p in range(pieces):
        out_ref[p, 0:share, :] = total[p * share : (p + 1) * share, :]
        out_ref[p, share:8, :] = total[comps : comps + 8 - share, :]


def gather_body(pixels, in_ref, out_ref):
    total = jnp.sum(in_ref[...], axis=0) / pixels
    for j in range(out_ref.shape[0]):
        out_ref[j] = total


def last_body(in_ref, load_ref, off_ref):
    pieces = in_ref.shape[0]
    share = load_ref.shape[0] // pieces
    for p in range(pieces):
        load_ref[p * share : (p + 1) * share, :] = in_ref[p, 0:share, :]
    off_ref[...] = in_ref[0, share : share + 1, :]


def on_device(counts, offset, loading):
    pixels = counts.shape[0] * lax.axis_size(WIDE)
    comps = loading.shape[1]
    channels = counts.shape[1] * PARTS * 2
    height = counts.shape[0] // 2 // PARTS + 8 + comps // PARTS
    core = lax.axis_index("c").astype(jnp.int32)
    side = lax.axis_index("zl").astype(jnp.int32).reshape(1)
    offset = offset.reshape(1, comps)

    swap = [(0, 1), (1, 0)]
    near_pairs = []
    for z in range(PARTS):
        for c in range(2):
            partner = (((z - c) % PARTS ^ 1) + c) % PARTS
            near_pairs.append((2 * z + c, 2 * partner + c))

    plane = lax.axis_size(WIDE)
    planes = [
        [2 * (PARTS * p + z) + c for p in (reversed(range(plane)) if c else range(plane))]
        for z in range(PARTS)
        for c in range(2)
    ]

    half = counts.shape[0] // 2
    scratch = [pltpu.VMEM((1, comps), F32), pltpu.SemaphoreType.DMA((4,))]
    sent = cut(send_body, half + comps + 8, scratch, 1 - core, counts, loading, offset)
    other = lax.ppermute(sent, "c", swap)
    mine = cut(keep_body, half, [pltpu.SemaphoreType.DMA], core, counts)
    block = whole(PARTS, height, comps)
    partial = call(encode_body, block, mine, loading, offset)
    partial = call(encode_last_body, block, partial, other)
    gathered = lax.all_to_all(partial, ("zh", "zl"), 0, 0)
    own = call(functools.partial(finish_body, channels), whole(height, comps), gathered)
    scores = lax.all_gather(own, "zh", axis=0)
    near = lax.ppermute(scores, DEEP, near_pairs)
    some = call(
        some_grad_body, whole(comps + 8, 3 * comps), side, scores, mine, other, offset, scalars=1
    )
    shape = whole(comps + 8, comps)
    grad_other, rest = call(
        grad_body, (shape, whole(5, comps, comps)), side, near, scores, some, mine, other, offset, scalars=1
    )
    arrived = lax.ppermute(grad_other, "c", swap)
    grad_mine = call(mine_grad_body, shape, rest, loading)
    pieces = call(deal_body, whole(plane, 8, comps), grad_mine, arrived)
    pieces = lax.all_to_all(pieces, AXES, 0, 0, axis_index_groups=planes)
    pieces = call(functools.partial(gather_body, pixels), whole(plane, 8, comps), pieces)
    pieces = lax.all_to_all(pieces, AXES, 0, 0, axis_index_groups=planes)
    grad, grad_offset = call(last_body, (whole(comps, comps), whole(1, comps)), pieces)
    return grad, grad_offset.reshape(comps)


def solution(mesh):
    wide, deep = mesh.devices.shape
    split_mesh = Mesh(mesh.devices.reshape(wide // 4, 4, deep // 4, 2, 2), AXES)
    return jax.shard_map(
        on_device,
        mesh=split_mesh,
        in_specs=(P(WIDE, DEEP), P(DEEP), P(DEEP, None)),
        out_specs=(P(DEEP, None), P(DEEP)),
        check_vma=False,
    )
```

```python
import functools

import jax
import jax.numpy as jnp
from jax import lax
from jax.experimental import pallas as pl
from jax.experimental.pallas import tpu as pltpu
from jax.sharding import Mesh
from jax.sharding import PartitionSpec as P

F32 = jnp.float32
AXES = ("y", "x", "zh", "zl", "c")
WIDE = ("y", "x")
DEEP = ("zh", "zl", "c")
PARTS = 8
LIMIT = 48 * 1024 * 1024


def mult(left, right, contract=((1,), (0,))):
    return lax.dot_general(
        left, right, (contract, ((), ())),
        preferred_element_type=F32, precision=lax.Precision.HIGHEST,
    )


def whole(*shape):
    return jax.ShapeDtypeStruct(shape, F32)


def call(body, out_shape, *args, scalars=0):
    spaces = [pltpu.SMEM] * scalars + [pltpu.VMEM] * (len(args) - scalars)
    return pl.pallas_call(
        body,
        out_shape=out_shape,
        in_specs=[pl.BlockSpec(memory_space=space) for space in spaces],
        compiler_params=pltpu.CompilerParams(vmem_limit_bytes=LIMIT),
    )(*args)


def send_body(which, counts_ref, loading_ref, offset_ref, out_ref, held, row, sems):
    rows, comps = held.shape
    half = rows // 2
    copies = [
        pltpu.make_async_copy(
            counts_ref.at[pl.ds(pl.multiple_of(which[0] * rows + k * half, half), half), :],
            held.at[pl.ds(k * half, half), :],
            sems.at[k],
        )
        for k in range(2)
    ]
    copies.append(pltpu.make_async_copy(loading_ref, out_ref.at[pl.ds(rows, comps), :], sems.at[2]))
    copies.append(pltpu.make_async_copy(offset_ref, row, sems.at[3]))
    for copy in copies:
        copy.start()
    for k in range(2):
        copies[k].wait()
        out_ref[k * half : (k + 1) * half, :] = jnp.log(held[k * half : (k + 1) * half, :])
    copies[2].wait()
    copies[3].wait()
    out_ref[rows + comps : rows + comps + 8, :] = jnp.broadcast_to(row[...], (8, comps))


def keep_body(which, counts_ref, out_ref, held, sem):
    rows = held.shape[0]
    copy = pltpu.make_async_copy(
        counts_ref.at[pl.ds(pl.multiple_of(which[0] * rows, rows), rows), :], held, sem
    )
    copy.start()
    copy.wait()
    out_ref[...] = jnp.log(held[...])


def cut(body, height, scratch, which, counts, *more):
    rows, width = counts.shape[0] // 2, counts.shape[1]
    return pl.pallas_call(
        body,
        out_shape=whole(height, width),
        in_specs=[pl.BlockSpec(memory_space=pltpu.SMEM)]
        + [pl.BlockSpec(memory_space=pltpu.HBM)] * (1 + len(more)),
        scratch_shapes=[pltpu.VMEM((rows, width), F32)] + scratch,
        compiler_params=pltpu.CompilerParams(vmem_limit_bytes=LIMIT),
    )(which.reshape(1), *(pltpu.with_memory_space_constraint(a, pltpu.HBM) for a in (counts,) + more))


def fold(gram):
    half = gram.shape[0] // 2
    row = lax.broadcasted_iota(jnp.int32, (half, 2 * half), 0)
    col = lax.broadcasted_iota(jnp.int32, (half, 2 * half), 1)
    low = pltpu.roll(gram[half:, :], half, 1)
    folded = jnp.where((col < half) & (col > row), low, gram[:half, :])
    return folded, jnp.sum(jnp.where(col == row, low, 0.0), axis=0, keepdims=True)


def unfold(folded, diagonal):
    half = folded.shape[0]
    row = lax.broadcasted_iota(jnp.int32, (half, 2 * half), 0)
    col = lax.broadcasted_iota(jnp.int32, (half, 2 * half), 1)
    turned = jnp.concatenate([folded, jnp.zeros_like(folded)], axis=0).T
    high = jnp.where((col < half) & (col > row), turned[:half, :], folded)
    right = jnp.where(
        col - half > row,
        pltpu.roll(folded, half, 1),
        pltpu.roll(jnp.where(col == row, diagonal, turned[:half, :]), half, 1),
    )
    return jnp.concatenate([high, jnp.where(col < half, turned[half:, :], right)], axis=0)


def source_terms(load, off):
    bar = jnp.sum(load, axis=0, keepdims=True) / load.shape[0]
    return bar, load - bar, mult(off, load)[0:1, :], fold(mult(load, load, ((0,), (0,))))


def log_sums(logs):
    comps = logs.shape[1]
    return [
        jnp.sum(logs[h * comps : (h + 1) * comps, :].T, axis=0, keepdims=True)
        for h in range(logs.shape[0] // comps)
    ]


def encode_body(mine, loading_ref, offset_ref, out_ref):
    total, comps = mine.shape
    rows, share = total // PARTS, comps // 2 // PARTS
    bar, bare, shift, (gram, diagonal) = source_terms(
        loading_ref[...], jnp.broadcast_to(offset_ref[...], (8, comps))
    )
    blank = jnp.zeros((1, comps), F32)
    for j in range(PARTS):
        logs = mine[j * rows : (j + 1) * rows, :]
        out_ref[j, 0:rows, :] = mult(logs, bare)
        out_ref[j, rows : rows + 8, :] = jnp.concatenate(
            log_sums(logs) + [blank, blank, bar, blank, shift, diagonal], axis=0
        )
        out_ref[j, rows + 8 : rows + 8 + share, :] = gram[j * share : (j + 1) * share, :]


def encode_last_body(in_ref, other, out_ref):
    height, comps = in_ref.shape[1:]
    share = comps // 2 // PARTS
    rows = height - 8 - share
    total = PARTS * rows
    bar, bare, shift, (gram, diagonal) = source_terms(
        other[total : total + comps, :], other[total + comps : total + comps + 8, :]
    )
    blank = jnp.zeros((1, comps), F32)
    for j in range(PARTS):
        logs = other[j * rows : (j + 1) * rows, :]
        out_ref[j, 0:rows, :] = in_ref[j, 0:rows, :] + mult(logs, bare)
        out_ref[j, rows : rows + 8, :] = in_ref[j, rows : rows + 8, :] + jnp.concatenate(
            [blank, blank] + log_sums(logs) + [blank, bar, shift, diagonal], axis=0
        )
        at = rows + 8
        out_ref[j, at : at + share, :] = in_ref[j, at : at + share, :] + gram[j * share : (j + 1) * share, :]


def finish_body(channels, in_ref, out_ref):
    height, comps = in_ref.shape[1:]
    share = comps // 2 // PARTS
    rows = height - 8 - share
    group = channels // (2 * PARTS)
    bars = jnp.concatenate([in_ref[j, rows + 4 : rows + 6, :] for j in range(PARTS)], axis=0)
    shift = sum(in_ref[j, rows + 6 : rows + 7, :] for j in range(PARTS))
    geos = []
    for h in range(2):
        sums = jnp.concatenate(
            [
                in_ref[j, rows + h + k : rows + h + k + 1, :]
                for j in range(PARTS)
                for k in (0, 2)
            ],
            axis=0,
        )
        geo = jnp.sum(sums, axis=0, keepdims=True) / channels
        at = h * comps
        total = mult(sums - group * geo, bars, ((0,), (0,))) - shift
        for j in range(PARTS):
            total += in_ref[j, at : at + comps, :]
        out_ref[at : at + comps, :] = total
        geos.append(geo)
    diagonal = sum(in_ref[j, rows + 7 : rows + 8, :] for j in range(PARTS))
    out_ref[rows : rows + 8, :] = jnp.concatenate(geos + [diagonal, jnp.zeros((5, comps), F32)], axis=0)
    out_ref[rows + 8 : rows + 8 + share, :] = sum(in_ref[j, rows + 8 : rows + 8 + share, :] for j in range(PARTS))


def block_terms(first, in_ref, logs, offs):
    blocks, height, comps = in_ref.shape
    rows = height - 8 - comps // 2 // PARTS
    wide, sums = 0.0, 0.0
    for j in range(blocks):
        s = in_ref[j, 0:rows, :]
        geo = jnp.concatenate(
            [
                jnp.broadcast_to(in_ref[j, rows + h : rows + h + 1, :], (comps, comps)).T
                for h in range(2)
            ],
            axis=0,
        )
        here = pl.ds(pl.multiple_of((2 * j + first) * rows, rows), rows)
        both = jnp.concatenate([a[here, :] - geo - off for a, off in zip(logs, offs)] + [s], axis=1)
        sums += jnp.sum(both, axis=0, keepdims=True)
        wide += mult(s.T, both)
    return wide, sums


def some_grad_body(side, in_ref, mine, other, offset_ref, out_ref):
    total, comps = mine.shape
    offs = (offset_ref[...], other[total + comps : total + comps + 1, :])
    wide, sums = block_terms(side[0], in_ref, (mine, other), offs)
    out_ref[0:comps, :] = wide
    out_ref[comps : comps + 8, :] = jnp.broadcast_to(sums, (8, sums.shape[1]))


def grad_body(side, near_ref, in_ref, some_ref, mine, other, offset_ref, out_ref, rest_ref):
    total, comps = mine.shape
    height = in_ref.shape[1]
    share = comps // 2 // PARTS
    rows = height - 8 - share
    offs = (offset_ref[...], other[total + comps : total + comps + 1, :])
    wide, sums = block_terms(1 - side[0], near_ref, (mine, other), offs)
    wide, sums = wide + some_ref[0:comps, :], sums + some_ref[comps : comps + 1, :]
    here = [a[j, rows + 8 : rows + 8 + share, :] for j in range(PARTS // 2) for a in (in_ref, near_ref)]
    there = [a[j, rows + 8 : rows + 8 + share, :] for j in range(PARTS // 2) for a in (near_ref, in_ref)]
    gram = jnp.where(side[0] == 0, jnp.concatenate(here, axis=0), jnp.concatenate(there, axis=0))
    gram = unfold(gram, in_ref[0, rows + 2 : rows + 3, :])
    row = lax.broadcasted_iota(jnp.int32, (comps, comps), 0)
    col = lax.broadcasted_iota(jnp.int32, (comps, comps), 1)
    hat = gram - jnp.where(row == col, 2.0, 0.0).astype(F32)
    square = wide[:, 2 * comps : 3 * comps]
    s_sum, c_mine, c_other = (sums[:, k * comps : (k + 1) * comps] for k in (2, 0, 1))
    source_grad(wide[:, comps : 2 * comps], hat, square, s_sum, c_other, other[total : total + comps, :], out_ref)
    rest_ref[0] = wide[:, 0:comps]
    rest_ref[1] = hat
    rest_ref[2] = square
    rest_ref[3] = jnp.broadcast_to(s_sum, (comps, comps))
    rest_ref[4] = jnp.broadcast_to(c_mine, (comps, comps))


def source_grad(w_turned, hat, square, s_sum, c_sum, load, out_ref):
    comps = load.shape[1]
    s_hat = mult(jnp.broadcast_to(s_sum, (8, comps)), hat)
    out_ref[0:comps, :] = mult(w_turned, hat, ((0,), (0,))) + mult(load, square)
    out_ref[comps : comps + 8, :] = -(mult(s_hat, load, ((1,), (1,))) + c_sum)


def mine_grad_body(rest_ref, loading_ref, out_ref):
    source_grad(
        rest_ref[0], rest_ref[1], rest_ref[2], rest_ref[3, 0:1, :], rest_ref[4, 0:1, :], loading_ref[...], out_ref
    )


def deal_body(a_ref, b_ref, out_ref):
    pieces, _, comps = out_ref.shape
    share = comps // pieces
    total = a_ref[...] + b_ref[...]
    for p in range(pieces):
        out_ref[p, 0:share, :] = total[p * share : (p + 1) * share, :]
        out_ref[p, share:8, :] = total[comps : comps + 8 - share, :]


def gather_body(pixels, in_ref, out_ref):
    total = jnp.sum(in_ref[...], axis=0) / pixels
    for j in range(out_ref.shape[0]):
        out_ref[j] = total


def last_body(in_ref, load_ref, off_ref):
    pieces = in_ref.shape[0]
    share = load_ref.shape[0] // pieces
    for p in range(pieces):
        load_ref[p * share : (p + 1) * share, :] = in_ref[p, 0:share, :]
    off_ref[...] = in_ref[0, share : share + 1, :]


def on_device(counts, offset, loading):
    pixels = counts.shape[0] * lax.axis_size(WIDE)
    comps = loading.shape[1]
    channels = counts.shape[1] * PARTS * 2
    height = counts.shape[0] // 2 // PARTS + 8 + comps // 2 // PARTS
    core = lax.axis_index("c").astype(jnp.int32)
    side = (lax.axis_index("zl") ^ lax.axis_index("c")).astype(jnp.int32).reshape(1)
    offset = offset.reshape(1, comps)

    swap = [(0, 1), (1, 0)]
    near_pairs = []
    for z in range(PARTS):
        for c in range(2):
            partner = (((z - c) % PARTS ^ 1) + c) % PARTS
            near_pairs.append((2 * z + c, 2 * partner + c))

    rings = [[2 * z for z in range(PARTS)], [2 * z + 1 for z in reversed(range(PARTS))]]
    rings4 = [ring[k::2] for ring in rings for k in range(2)]
    plane = lax.axis_size(WIDE)
    planes = [
        [2 * (PARTS * p + z) + c for p in (reversed(range(plane)) if c else range(plane))]
        for z in range(PARTS)
        for c in range(2)
    ]

    half = counts.shape[0] // 2
    scratch = [pltpu.VMEM((1, comps), F32), pltpu.SemaphoreType.DMA((4,))]
    sent = cut(send_body, half + comps + 8, scratch, 1 - core, counts, loading, offset)
    other = lax.ppermute(sent, "c", swap)
    mine = cut(keep_body, half, [pltpu.SemaphoreType.DMA], core, counts)
    block = whole(PARTS, height, comps)
    partial = call(encode_body, block, mine, loading, offset)
    partial = call(encode_last_body, block, partial, other)
    gathered = lax.all_to_all(partial, DEEP, 0, 0, axis_index_groups=rings)
    own = call(functools.partial(finish_body, channels), whole(height, comps), gathered)
    scores = lax.all_gather(own, DEEP, axis=0, axis_index_groups=rings4)
    near = lax.ppermute(scores, DEEP, near_pairs)
    some = call(
        some_grad_body, whole(comps + 8, 3 * comps), side, scores, mine, other, offset, scalars=1
    )
    shape = whole(comps + 8, comps)
    grad_other, rest = call(
        grad_body, (shape, whole(5, comps, comps)), side, near, scores, some, mine, other, offset, scalars=1
    )
    arrived = lax.ppermute(grad_other, "c", swap)
    grad_mine = call(mine_grad_body, shape, rest, loading)
    pieces = call(deal_body, whole(plane, 8, comps), grad_mine, arrived)
    pieces = lax.all_to_all(pieces, AXES, 0, 0, axis_index_groups=planes)
    pieces = call(functools.partial(gather_body, pixels), whole(plane, 8, comps), pieces)
    pieces = lax.all_to_all(pieces, AXES, 0, 0, axis_index_groups=planes)
    grad, grad_offset = call(last_body, (whole(comps, comps), whole(1, comps)), pieces)
    return grad, grad_offset.reshape(comps)


def solution(mesh):
    wide, deep = mesh.devices.shape
    split_mesh = Mesh(mesh.devices.reshape(wide // 4, 4, deep // 4, 2, 2), AXES)
    return jax.shard_map(
        on_device,
        mesh=split_mesh,
        in_specs=(P(WIDE, DEEP), P(DEEP), P(DEEP, None)),
        out_specs=(P(DEEP, None), P(DEEP)),
        check_vma=False,
    )
```

```python
import functools

import jax
import jax.numpy as jnp
from jax import lax
from jax.experimental import pallas as pl
from jax.experimental.pallas import tpu as pltpu
from jax.sharding import Mesh
from jax.sharding import PartitionSpec as P

F32 = jnp.float32
AXES = ("y", "x", "zh", "zl", "c")
WIDE = ("y", "x")
DEEP = ("zh", "zl", "c")
PARTS = 8
LIMIT = 48 * 1024 * 1024


def mult(left, right, contract=((1,), (0,))):
    return lax.dot_general(
        left, right, (contract, ((), ())),
        preferred_element_type=F32, precision=lax.Precision.HIGHEST,
    )


def whole(*shape):
    return jax.ShapeDtypeStruct(shape, F32)


def call(body, out_shape, *args, scalars=0):
    spaces = [pltpu.SMEM] * scalars + [pltpu.VMEM] * (len(args) - scalars)
    return pl.pallas_call(
        body,
        out_shape=out_shape,
        in_specs=[pl.BlockSpec(memory_space=space) for space in spaces],
        compiler_params=pltpu.CompilerParams(vmem_limit_bytes=LIMIT),
    )(*args)


def send_body(which, counts_ref, loading_ref, offset_ref, out_ref, held, row, sems):
    rows, comps = held.shape
    half = rows // 2
    copies = [
        pltpu.make_async_copy(
            counts_ref.at[pl.ds(pl.multiple_of(which[0] * rows + k * half, half), half), :],
            held.at[pl.ds(k * half, half), :],
            sems.at[k],
        )
        for k in range(2)
    ]
    copies.append(pltpu.make_async_copy(loading_ref, out_ref.at[pl.ds(rows, comps), :], sems.at[2]))
    copies.append(pltpu.make_async_copy(offset_ref, row, sems.at[3]))
    for copy in copies:
        copy.start()
    for k in range(2):
        copies[k].wait()
        out_ref[k * half : (k + 1) * half, :] = jnp.log(held[k * half : (k + 1) * half, :])
    copies[2].wait()
    copies[3].wait()
    out_ref[rows + comps : rows + comps + 8, :] = jnp.broadcast_to(row[...], (8, comps))


def keep_body(which, counts_ref, out_ref, held, sem):
    rows = held.shape[0]
    copy = pltpu.make_async_copy(
        counts_ref.at[pl.ds(pl.multiple_of(which[0] * rows, rows), rows), :], held, sem
    )
    copy.start()
    copy.wait()
    out_ref[...] = jnp.log(held[...])


def cut(body, height, scratch, which, counts, *more):
    rows, width = counts.shape[0] // 2, counts.shape[1]
    return pl.pallas_call(
        body,
        out_shape=whole(height, width),
        in_specs=[pl.BlockSpec(memory_space=pltpu.SMEM)]
        + [pl.BlockSpec(memory_space=pltpu.HBM)] * (1 + len(more)),
        scratch_shapes=[pltpu.VMEM((rows, width), F32)] + scratch,
        compiler_params=pltpu.CompilerParams(vmem_limit_bytes=LIMIT),
    )(which.reshape(1), *(pltpu.with_memory_space_constraint(a, pltpu.HBM) for a in (counts,) + more))


def fold(gram):
    half = gram.shape[0] // 2
    row = lax.broadcasted_iota(jnp.int32, (half, 2 * half), 0)
    col = lax.broadcasted_iota(jnp.int32, (half, 2 * half), 1)
    low = pltpu.roll(gram[half:, :], half, 1)
    folded = jnp.where((col < half) & (col > row), low, gram[:half, :])
    return folded, jnp.sum(jnp.where(col == row, low, 0.0), axis=0, keepdims=True)


def unfold(folded, diagonal):
    half = folded.shape[0]
    row = lax.broadcasted_iota(jnp.int32, (half, 2 * half), 0)
    col = lax.broadcasted_iota(jnp.int32, (half, 2 * half), 1)
    turned = jnp.concatenate([folded, jnp.zeros_like(folded)], axis=0).T
    high = jnp.where((col < half) & (col > row), turned[:half, :], folded)
    right = jnp.where(
        col - half > row,
        pltpu.roll(folded, half, 1),
        pltpu.roll(jnp.where(col == row, diagonal, turned[:half, :]), half, 1),
    )
    return jnp.concatenate([high, jnp.where(col < half, turned[half:, :], right)], axis=0)


def source_terms(load, off):
    bar = jnp.sum(load, axis=0, keepdims=True) / load.shape[0]
    return bar, load - bar, mult(off, load)[0:1, :], fold(mult(load, load, ((0,), (0,))))


def log_sums(logs):
    comps = logs.shape[1]
    return [
        jnp.sum(logs[h * comps : (h + 1) * comps, :].T, axis=0, keepdims=True)
        for h in range(logs.shape[0] // comps)
    ]


def encode_body(mine, loading_ref, offset_ref, out_ref):
    total, comps = mine.shape
    rows, share = total // PARTS, comps // 2 // PARTS
    bar, bare, shift, (gram, diagonal) = source_terms(
        loading_ref[...], jnp.broadcast_to(offset_ref[...], (8, comps))
    )
    blank = jnp.zeros((1, comps), F32)
    for j in range(PARTS):
        logs = mine[j * rows : (j + 1) * rows, :]
        out_ref[j, 0:rows, :] = mult(logs, bare)
        out_ref[j, rows : rows + 8, :] = jnp.concatenate(
            log_sums(logs) + [blank, blank, bar, blank, shift, diagonal], axis=0
        )
        out_ref[j, rows + 8 : rows + 8 + share, :] = gram[j * share : (j + 1) * share, :]


def encode_last_body(in_ref, other, out_ref):
    height, comps = in_ref.shape[1:]
    share = comps // 2 // PARTS
    rows = height - 8 - share
    total = PARTS * rows
    bar, bare, shift, (gram, diagonal) = source_terms(
        other[total : total + comps, :], other[total + comps : total + comps + 8, :]
    )
    blank = jnp.zeros((1, comps), F32)
    for j in range(PARTS):
        logs = other[j * rows : (j + 1) * rows, :]
        out_ref[j, 0:rows, :] = in_ref[j, 0:rows, :] + mult(logs, bare)
        out_ref[j, rows : rows + 8, :] = in_ref[j, rows : rows + 8, :] + jnp.concatenate(
            [blank, blank] + log_sums(logs) + [blank, bar, shift, diagonal], axis=0
        )
        at = rows + 8
        out_ref[j, at : at + share, :] = in_ref[j, at : at + share, :] + gram[j * share : (j + 1) * share, :]


def finish_body(channels, in_ref, out_ref):
    height, comps = in_ref.shape[1:]
    share = comps // 2 // PARTS
    rows = height - 8 - share
    group = channels // (2 * PARTS)
    bars = jnp.concatenate([in_ref[j, rows + 4 : rows + 6, :] for j in range(PARTS)], axis=0)
    shift = sum(in_ref[j, rows + 6 : rows + 7, :] for j in range(PARTS))
    geos = []
    for h in range(2):
        sums = jnp.concatenate(
            [
                in_ref[j, rows + h + k : rows + h + k + 1, :]
                for j in range(PARTS)
                for k in (0, 2)
            ],
            axis=0,
        )
        geo = jnp.sum(sums, axis=0, keepdims=True) / channels
        at = h * comps
        total = mult(sums - group * geo, bars, ((0,), (0,))) - shift
        for j in range(PARTS):
            total += in_ref[j, at : at + comps, :]
        out_ref[at : at + comps, :] = total
        geos.append(geo)
    diagonal = sum(in_ref[j, rows + 7 : rows + 8, :] for j in range(PARTS))
    out_ref[rows : rows + 8, :] = jnp.concatenate(geos + [diagonal, jnp.zeros((5, comps), F32)], axis=0)
    out_ref[rows + 8 : rows + 8 + share, :] = sum(in_ref[j, rows + 8 : rows + 8 + share, :] for j in range(PARTS))


def block_terms(first, in_ref, logs, offs):
    blocks, height, comps = in_ref.shape
    rows = height - 8 - comps // 2 // PARTS
    wide, sums = 0.0, 0.0
    for j in range(blocks):
        s = in_ref[j, 0:rows, :]
        geo = jnp.concatenate(
            [
                jnp.broadcast_to(in_ref[j, rows + h : rows + h + 1, :], (comps, comps)).T
                for h in range(2)
            ],
            axis=0,
        )
        here = pl.ds(pl.multiple_of((2 * j + first) * rows, rows), rows)
        both = jnp.concatenate([a[here, :] - geo - off for a, off in zip(logs, offs)] + [s], axis=1)
        sums += jnp.sum(both, axis=0, keepdims=True)
        wide += mult(s.T, both)
    return wide, sums


def some_grad_body(side, in_ref, mine, other, offset_ref, out_ref):
    total, comps = mine.shape
    offs = (offset_ref[...], other[total + comps : total + comps + 1, :])
    wide, sums = block_terms(side[0], in_ref, (mine, other), offs)
    out_ref[0:comps, :] = wide
    out_ref[comps : comps + 8, :] = jnp.broadcast_to(sums, (8, sums.shape[1]))


def grad_body(side, near_ref, in_ref, some_ref, mine, other, offset_ref, out_ref, rest_ref):
    total, comps = mine.shape
    height = in_ref.shape[1]
    share = comps // 2 // PARTS
    rows = height - 8 - share
    offs = (offset_ref[...], other[total + comps : total + comps + 1, :])
    wide, sums = block_terms(1 - side[0], near_ref, (mine, other), offs)
    wide, sums = wide + some_ref[0:comps, :], sums + some_ref[comps : comps + 1, :]
    here = [a[j, rows + 8 : rows + 8 + share, :] for j in range(PARTS // 2) for a in (in_ref, near_ref)]
    there = [a[j, rows + 8 : rows + 8 + share, :] for j in range(PARTS // 2) for a in (near_ref, in_ref)]
    gram = jnp.where(side[0] == 0, jnp.concatenate(here, axis=0), jnp.concatenate(there, axis=0))
    gram = unfold(gram, in_ref[0, rows + 2 : rows + 3, :])
    row = lax.broadcasted_iota(jnp.int32, (comps, comps), 0)
    col = lax.broadcasted_iota(jnp.int32, (comps, comps), 1)
    hat = gram - jnp.where(row == col, 2.0, 0.0).astype(F32)
    square = wide[:, 2 * comps : 3 * comps]
    s_sum, c_mine, c_other = (sums[:, k * comps : (k + 1) * comps] for k in (2, 0, 1))
    source_grad(wide[:, comps : 2 * comps], hat, square, s_sum, c_other, other[total : total + comps, :], out_ref)
    rest_ref[0] = wide[:, 0:comps]
    rest_ref[1] = hat
    rest_ref[2] = square
    rest_ref[3] = jnp.broadcast_to(s_sum, (comps, comps))
    rest_ref[4] = jnp.broadcast_to(c_mine, (comps, comps))


def source_grad(w_turned, hat, square, s_sum, c_sum, load, out_ref):
    comps = load.shape[1]
    s_hat = mult(jnp.broadcast_to(s_sum, (8, comps)), hat)
    out_ref[0:comps, :] = mult(w_turned, hat, ((0,), (0,))) + mult(load, square)
    out_ref[comps : comps + 8, :] = -(mult(s_hat, load, ((1,), (1,))) + c_sum)


def mine_grad_body(rest_ref, loading_ref, out_ref):
    source_grad(
        rest_ref[0], rest_ref[1], rest_ref[2], rest_ref[3, 0:1, :], rest_ref[4, 0:1, :], loading_ref[...], out_ref
    )


def deal_body(a_ref, b_ref, out_ref):
    pieces, _, comps = out_ref.shape
    share = comps // pieces
    total = a_ref[...] + b_ref[...]
    for p in range(pieces):
        out_ref[p, 0:share, :] = total[p * share : (p + 1) * share, :]
        out_ref[p, share:8, :] = total[comps : comps + 8 - share, :]


def gather_body(pixels, in_ref, out_ref):
    total = jnp.sum(in_ref[...], axis=0) / pixels
    for j in range(out_ref.shape[0]):
        out_ref[j] = total


def last_body(in_ref, load_ref, off_ref):
    pieces = in_ref.shape[0]
    share = load_ref.shape[0] // pieces
    for p in range(pieces):
        load_ref[p * share : (p + 1) * share, :] = in_ref[p, 0:share, :]
    off_ref[...] = in_ref[0, share : share + 1, :]


def on_device(counts, offset, loading):
    pixels = counts.shape[0] * lax.axis_size(WIDE)
    comps = loading.shape[1]
    channels = counts.shape[1] * PARTS * 2
    height = counts.shape[0] // 2 // PARTS + 8 + comps // 2 // PARTS
    core = lax.axis_index("c").astype(jnp.int32)
    side = lax.axis_index("zl").astype(jnp.int32).reshape(1)
    offset = offset.reshape(1, comps)

    swap = [(0, 1), (1, 0)]
    near_pairs = []
    for z in range(PARTS):
        for c in range(2):
            partner = (((z - c) % PARTS ^ 1) + c) % PARTS
            near_pairs.append((2 * z + c, 2 * partner + c))

    rings = [[2 * (step * k % PARTS) + c for k in range(PARTS)] for c, step in ((0, 3), (1, PARTS - 3))]
    rings4 = [ring[k::2] for ring in rings for k in range(2)]
    plane = lax.axis_size(WIDE)
    planes = [
        [2 * (PARTS * (step * k % plane) + z) + c for k in range(plane)]
        for z in range(PARTS)
        for c, step in ((0, 11), (1, plane - 11))
    ]

    half = counts.shape[0] // 2
    scratch = [pltpu.VMEM((1, comps), F32), pltpu.SemaphoreType.DMA((4,))]
    sent = cut(send_body, half + comps + 8, scratch, 1 - core, counts, loading, offset)
    other = lax.ppermute(sent, "c", swap)
    mine = cut(keep_body, half, [pltpu.SemaphoreType.DMA], core, counts)
    block = whole(PARTS, height, comps)
    partial = call(encode_body, block, mine, loading, offset)
    partial = call(encode_last_body, block, partial, other)
    gathered = lax.all_to_all(partial, DEEP, 0, 0, axis_index_groups=rings)
    own = call(functools.partial(finish_body, channels), whole(height, comps), gathered)
    scores = lax.all_gather(own, DEEP, axis=0, axis_index_groups=rings4)
    near = lax.ppermute(scores, DEEP, near_pairs)
    some = call(
        some_grad_body, whole(comps + 8, 3 * comps), side, scores, mine, other, offset, scalars=1
    )
    shape = whole(comps + 8, comps)
    grad_other, rest = call(
        grad_body, (shape, whole(5, comps, comps)), side, near, scores, some, mine, other, offset, scalars=1
    )
    arrived = lax.ppermute(grad_other, "c", swap)
    grad_mine = call(mine_grad_body, shape, rest, loading)
    pieces = call(deal_body, whole(plane, 8, comps), grad_mine, arrived)
    pieces = lax.all_to_all(pieces, AXES, 0, 0, axis_index_groups=planes)
    pieces = call(functools.partial(gather_body, pixels), whole(plane, 8, comps), pieces)
    pieces = lax.all_to_all(pieces, AXES, 0, 0, axis_index_groups=planes)
    grad, grad_offset = call(last_body, (whole(comps, comps), whole(1, comps)), pieces)
    return grad, grad_offset.reshape(comps)


def solution(mesh):
    wide, deep = mesh.devices.shape
    split_mesh = Mesh(mesh.devices.reshape(wide // 4, 4, deep // 4, 2, 2), AXES)
    return jax.shard_map(
        on_device,
        mesh=split_mesh,
        in_specs=(P(WIDE, DEEP), P(DEEP), P(DEEP, None)),
        out_specs=(P(DEEP, None), P(DEEP)),
        check_vma=False,
    )
```

```python
import functools

import jax
import jax.numpy as jnp
from jax import lax
from jax.experimental import pallas as pl
from jax.experimental.pallas import tpu as pltpu
from jax.sharding import Mesh
from jax.sharding import PartitionSpec as P

F32 = jnp.float32
AXES = ("y", "x", "zh", "zl", "c")
WIDE = ("y", "x")
DEEP = ("zh", "zl", "c")
PARTS = 8
LIMIT = 48 * 1024 * 1024


def mult(left, right, contract=((1,), (0,))):
    return lax.dot_general(
        left, right, (contract, ((), ())),
        preferred_element_type=F32, precision=lax.Precision.HIGHEST,
    )


def whole(*shape):
    return jax.ShapeDtypeStruct(shape, F32)


def call(body, out_shape, *args, scalars=0):
    spaces = [pltpu.SMEM] * scalars + [pltpu.VMEM] * (len(args) - scalars)
    return pl.pallas_call(
        body,
        out_shape=out_shape,
        in_specs=[pl.BlockSpec(memory_space=space) for space in spaces],
        compiler_params=pltpu.CompilerParams(vmem_limit_bytes=LIMIT),
    )(*args)


def send_body(which, counts_ref, loading_ref, offset_ref, out_ref, held, row, sems):
    rows, comps = held.shape
    half = rows // 2
    copies = [
        pltpu.make_async_copy(
            counts_ref.at[pl.ds(pl.multiple_of(which[0] * rows + k * half, half), half), :],
            held.at[pl.ds(k * half, half), :],
            sems.at[k],
        )
        for k in range(2)
    ]
    copies.append(pltpu.make_async_copy(loading_ref, out_ref.at[pl.ds(rows, comps), :], sems.at[2]))
    copies.append(pltpu.make_async_copy(offset_ref, row, sems.at[3]))
    for copy in copies:
        copy.start()
    for k in range(2):
        copies[k].wait()
        out_ref[k * half : (k + 1) * half, :] = jnp.log(held[k * half : (k + 1) * half, :])
    copies[2].wait()
    copies[3].wait()
    out_ref[rows + comps : rows + comps + 8, :] = jnp.broadcast_to(row[...], (8, comps))


def keep_body(which, counts_ref, out_ref, held, sem):
    rows = held.shape[0]
    copy = pltpu.make_async_copy(
        counts_ref.at[pl.ds(pl.multiple_of(which[0] * rows, rows), rows), :], held, sem
    )
    copy.start()
    copy.wait()
    out_ref[...] = jnp.log(held[...])


def cut(body, height, scratch, which, counts, *more):
    rows, width = counts.shape[0] // 2, counts.shape[1]
    return pl.pallas_call(
        body,
        out_shape=whole(height, width),
        in_specs=[pl.BlockSpec(memory_space=pltpu.SMEM)]
        + [pl.BlockSpec(memory_space=pltpu.HBM)] * (1 + len(more)),
        scratch_shapes=[pltpu.VMEM((rows, width), F32)] + scratch,
        compiler_params=pltpu.CompilerParams(vmem_limit_bytes=LIMIT),
    )(which.reshape(1), *(pltpu.with_memory_space_constraint(a, pltpu.HBM) for a in (counts,) + more))


def fold(gram):
    half = gram.shape[0] // 2
    row = lax.broadcasted_iota(jnp.int32, (half, 2 * half), 0)
    col = lax.broadcasted_iota(jnp.int32, (half, 2 * half), 1)
    low = pltpu.roll(gram[half:, :], half, 1)
    folded = jnp.where((col < half) & (col > row), low, gram[:half, :])
    return folded, jnp.sum(jnp.where(col == row, low, 0.0), axis=0, keepdims=True)


def unfold(folded, diagonal):
    half = folded.shape[0]
    row = lax.broadcasted_iota(jnp.int32, (half, 2 * half), 0)
    col = lax.broadcasted_iota(jnp.int32, (half, 2 * half), 1)
    turned = jnp.concatenate([folded, jnp.zeros_like(folded)], axis=0).T
    high = jnp.where((col < half) & (col > row), turned[:half, :], folded)
    right = jnp.where(
        col - half > row,
        pltpu.roll(folded, half, 1),
        pltpu.roll(jnp.where(col == row, diagonal, turned[:half, :]), half, 1),
    )
    return jnp.concatenate([high, jnp.where(col < half, turned[half:, :], right)], axis=0)


def source_terms(load, off):
    bar = jnp.sum(load, axis=0, keepdims=True) / load.shape[0]
    return bar, load - bar, mult(off, load)[0:1, :], fold(mult(load, load, ((0,), (0,))))


def log_sums(logs):
    comps = logs.shape[1]
    return [
        jnp.sum(logs[h * comps : (h + 1) * comps, :].T, axis=0, keepdims=True)
        for h in range(logs.shape[0] // comps)
    ]


def encode_body(mine, loading_ref, offset_ref, out_ref):
    total, comps = mine.shape
    rows, share = total // PARTS, comps // 2 // PARTS
    bar, bare, shift, (gram, diagonal) = source_terms(
        loading_ref[...], jnp.broadcast_to(offset_ref[...], (8, comps))
    )
    blank = jnp.zeros((1, comps), F32)
    for j in range(PARTS):
        logs = mine[j * rows : (j + 1) * rows, :]
        out_ref[j, 0:rows, :] = mult(logs, bare)
        out_ref[j, rows : rows + 8, :] = jnp.concatenate(
            log_sums(logs) + [blank, blank, bar, blank, shift, diagonal], axis=0
        )
        out_ref[j, rows + 8 : rows + 8 + share, :] = gram[j * share : (j + 1) * share, :]


def encode_last_body(in_ref, other, out_ref):
    height, comps = in_ref.shape[1:]
    share = comps // 2 // PARTS
    rows = height - 8 - share
    total = PARTS * rows
    bar, bare, shift, (gram, diagonal) = source_terms(
        other[total : total + comps, :], other[total + comps : total + comps + 8, :]
    )
    blank = jnp.zeros((1, comps), F32)
    for j in range(PARTS):
        logs = other[j * rows : (j + 1) * rows, :]
        out_ref[j, 0:rows, :] = in_ref[j, 0:rows, :] + mult(logs, bare)
        out_ref[j, rows : rows + 8, :] = in_ref[j, rows : rows + 8, :] + jnp.concatenate(
            [blank, blank] + log_sums(logs) + [blank, bar, shift, diagonal], axis=0
        )
        at = rows + 8
        out_ref[j, at : at + share, :] = in_ref[j, at : at + share, :] + gram[j * share : (j + 1) * share, :]


def finish_body(channels, in_ref, out_ref):
    height, comps = in_ref.shape[1:]
    share = comps // 2 // PARTS
    rows = height - 8 - share
    group = channels // (2 * PARTS)
    bars = jnp.concatenate([in_ref[j, rows + 4 : rows + 6, :] for j in range(PARTS)], axis=0)
    shift = sum(in_ref[j, rows + 6 : rows + 7, :] for j in range(PARTS))
    geos = []
    for h in range(2):
        sums = jnp.concatenate(
            [
                in_ref[j, rows + h + k : rows + h + k + 1, :]
                for j in range(PARTS)
                for k in (0, 2)
            ],
            axis=0,
        )
        geo = jnp.sum(sums, axis=0, keepdims=True) / channels
        at = h * comps
        total = mult(sums - group * geo, bars, ((0,), (0,))) - shift
        for j in range(PARTS):
            total += in_ref[j, at : at + comps, :]
        out_ref[at : at + comps, :] = total
        geos.append(geo)
    diagonal = sum(in_ref[j, rows + 7 : rows + 8, :] for j in range(PARTS))
    out_ref[rows : rows + 8, :] = jnp.concatenate(geos + [diagonal, jnp.zeros((5, comps), F32)], axis=0)
    out_ref[rows + 8 : rows + 8 + share, :] = sum(in_ref[j, rows + 8 : rows + 8 + share, :] for j in range(PARTS))


def block_terms(first, base, in_ref, logs, offs):
    blocks, height, comps = in_ref.shape
    rows = height - 8 - comps // 2 // PARTS
    wide, sums = 0.0, 0.0
    for j in range(blocks):
        s = in_ref[j, 0:rows, :]
        geo = jnp.concatenate(
            [
                jnp.broadcast_to(in_ref[j, rows + h : rows + h + 1, :], (comps, comps)).T
                for h in range(2)
            ],
            axis=0,
        )
        here = pl.ds(pl.multiple_of((2 * (base + j) + first) * rows, rows), rows)
        both = jnp.concatenate([a[here, :] - geo - off for a, off in zip(logs, offs)] + [s], axis=1)
        sums += jnp.sum(both, axis=0, keepdims=True)
        wide += mult(s.T, both)
    return wide, sums


def some_grad_body(other_side, side, in_ref, mine, other, offset_ref, *refs):
    total, comps = mine.shape
    out_ref = refs[-1]
    offs = (offset_ref[...], other[total + comps : total + comps + 1, :])
    first = 1 - side[0] if other_side else side[0]
    wide, sums = block_terms(first, 0, in_ref, (mine, other), offs)
    for before in refs[:-1]:
        wide, sums = wide + before[0:comps, :], sums + before[comps : comps + 1, :]
    out_ref[0:comps, :] = wide
    out_ref[comps : comps + 8, :] = jnp.broadcast_to(sums, (8, sums.shape[1]))


def grad_body(side, late_ref, early_ref, in_ref, some_ref, mine, other, offset_ref, out_ref, rest_ref):
    total, comps = mine.shape
    height = in_ref.shape[1]
    share = comps // 2 // PARTS
    rows = height - 8 - share
    offs = (offset_ref[...], other[total + comps : total + comps + 1, :])
    wide, sums = block_terms(1 - side[0], early_ref.shape[0], late_ref, (mine, other), offs)
    wide, sums = wide + some_ref[0:comps, :], sums + some_ref[comps : comps + 1, :]
    ours = [in_ref[j, rows + 8 : rows + 8 + share, :] for j in range(PARTS // 2)]
    theirs = [a[j, rows + 8 : rows + 8 + share, :] for a in (early_ref, late_ref) for j in range(PARTS // 4)]
    here = [a for pair in zip(ours, theirs) for a in pair]
    there = [a for pair in zip(theirs, ours) for a in pair]
    gram = jnp.where(side[0] == 0, jnp.concatenate(here, axis=0), jnp.concatenate(there, axis=0))
    gram = unfold(gram, in_ref[0, rows + 2 : rows + 3, :])
    row = lax.broadcasted_iota(jnp.int32, (comps, comps), 0)
    col = lax.broadcasted_iota(jnp.int32, (comps, comps), 1)
    hat = gram - jnp.where(row == col, 2.0, 0.0).astype(F32)
    square = wide[:, 2 * comps : 3 * comps]
    s_sum, c_mine, c_other = (sums[:, k * comps : (k + 1) * comps] for k in (2, 0, 1))
    source_grad(wide[:, comps : 2 * comps], hat, square, s_sum, c_other, other[total : total + comps, :], out_ref)
    rest_ref[0] = wide[:, 0:comps]
    rest_ref[1] = hat
    rest_ref[2] = square
    rest_ref[3] = jnp.broadcast_to(s_sum, (comps, comps))
    rest_ref[4] = jnp.broadcast_to(c_mine, (comps, comps))


def source_grad(w_turned, hat, square, s_sum, c_sum, load, out_ref):
    comps = load.shape[1]
    s_hat = mult(jnp.broadcast_to(s_sum, (8, comps)), hat)
    out_ref[0:comps, :] = mult(w_turned, hat, ((0,), (0,))) + mult(load, square)
    out_ref[comps : comps + 8, :] = -(mult(s_hat, load, ((1,), (1,))) + c_sum)


def mine_grad_body(rest_ref, loading_ref, out_ref):
    source_grad(
        rest_ref[0], rest_ref[1], rest_ref[2], rest_ref[3, 0:1, :], rest_ref[4, 0:1, :], loading_ref[...], out_ref
    )


def deal_body(a_ref, b_ref, out_ref):
    pieces, _, comps = out_ref.shape
    share = comps // pieces
    total = a_ref[...] + b_ref[...]
    for p in range(pieces):
        out_ref[p, 0:share, :] = total[p * share : (p + 1) * share, :]
        out_ref[p, share:8, :] = total[comps : comps + 8 - share, :]


def gather_body(pixels, in_ref, out_ref):
    total = jnp.sum(in_ref[...], axis=0) / pixels
    for j in range(out_ref.shape[0]):
        out_ref[j] = total


def last_body(in_ref, load_ref, off_ref):
    pieces = in_ref.shape[0]
    share = load_ref.shape[0] // pieces
    for p in range(pieces):
        load_ref[p * share : (p + 1) * share, :] = in_ref[p, 0:share, :]
    off_ref[...] = in_ref[0, share : share + 1, :]


def on_device(counts, offset, loading):
    pixels = counts.shape[0] * lax.axis_size(WIDE)
    comps = loading.shape[1]
    channels = counts.shape[1] * PARTS * 2
    height = counts.shape[0] // 2 // PARTS + 8 + comps // 2 // PARTS
    core = lax.axis_index("c").astype(jnp.int32)
    side = (lax.axis_index("zl") ^ lax.axis_index("c")).astype(jnp.int32).reshape(1)
    offset = offset.reshape(1, comps)

    swap = [(0, 1), (1, 0)]
    near_pairs = []
    for z in range(PARTS):
        for c in range(2):
            partner = (((z - c) % PARTS ^ 1) + c) % PARTS
            near_pairs.append((2 * z + c, 2 * partner + c))

    rings = [[2 * z for z in range(PARTS)], [2 * z + 1 for z in reversed(range(PARTS))]]
    rings4 = [ring[k::2] for ring in rings for k in range(2)]
    plane = lax.axis_size(WIDE)
    planes = [
        [2 * (PARTS * p + z) + c for p in (reversed(range(plane)) if c else range(plane))]
        for z in range(PARTS)
        for c in range(2)
    ]

    half = counts.shape[0] // 2
    scratch = [pltpu.VMEM((1, comps), F32), pltpu.SemaphoreType.DMA((4,))]
    sent = cut(send_body, half + comps + 8, scratch, 1 - core, counts, loading, offset)
    other = lax.ppermute(sent, "c", swap)
    mine = cut(keep_body, half, [pltpu.SemaphoreType.DMA], core, counts)
    block = whole(PARTS, height, comps)
    partial = call(encode_body, block, mine, loading, offset)
    partial = call(encode_last_body, block, partial, other)
    gathered = lax.all_to_all(partial, DEEP, 0, 0, axis_index_groups=rings)
    own = call(functools.partial(finish_body, channels), whole(height, comps), gathered)
    scores = lax.all_gather(own, DEEP, axis=0, axis_index_groups=rings4)
    early = lax.ppermute(scores[: PARTS // 4], DEEP, near_pairs)
    late = lax.ppermute(scores[PARTS // 4 :], DEEP, near_pairs)
    total = whole(comps + 8, 3 * comps)
    logs = (mine, other, offset)
    some = call(functools.partial(some_grad_body, False), total, side, scores, *logs, scalars=1)
    some = call(functools.partial(some_grad_body, True), total, side, early, *logs, some, scalars=1)
    shape = whole(comps + 8, comps)
    grad_other, rest = call(
        grad_body, (shape, whole(5, comps, comps)), side, late, early, scores, some, *logs, scalars=1
    )
    arrived = lax.ppermute(grad_other, "c", swap)
    grad_mine = call(mine_grad_body, shape, rest, loading)
    pieces = call(deal_body, whole(plane, 8, comps), grad_mine, arrived)
    pieces = lax.all_to_all(pieces, AXES, 0, 0, axis_index_groups=planes)
    pieces = call(functools.partial(gather_body, pixels), whole(plane, 8, comps), pieces)
    pieces = lax.all_to_all(pieces, AXES, 0, 0, axis_index_groups=planes)
    grad, grad_offset = call(last_body, (whole(comps, comps), whole(1, comps)), pieces)
    return grad, grad_offset.reshape(comps)


def solution(mesh):
    wide, deep = mesh.devices.shape
    split_mesh = Mesh(mesh.devices.reshape(wide // 4, 4, deep // 4, 2, 2), AXES)
    return jax.shard_map(
        on_device,
        mesh=split_mesh,
        in_specs=(P(WIDE, DEEP), P(DEEP), P(DEEP, None)),
        out_specs=(P(DEEP, None), P(DEEP)),
        check_vma=False,
    )
```

```python
import functools

import jax
import jax.numpy as jnp
from jax import lax
from jax.experimental import pallas as pl
from jax.experimental.pallas import tpu as pltpu
from jax.sharding import Mesh
from jax.sharding import PartitionSpec as P

F32 = jnp.float32
AXES = ("y", "x", "zh", "zl", "c")
WIDE = ("y", "x")
DEEP = ("zh", "zl", "c")
PARTS = 8
LIMIT = 48 * 1024 * 1024


def mult(left, right, contract=((1,), (0,))):
    return lax.dot_general(
        left, right, (contract, ((), ())),
        preferred_element_type=F32, precision=lax.Precision.HIGHEST,
    )


def whole(*shape):
    return jax.ShapeDtypeStruct(shape, F32)


def call(body, out_shape, *args, scalars=0):
    spaces = [pltpu.SMEM] * scalars + [pltpu.VMEM] * (len(args) - scalars)
    return pl.pallas_call(
        body,
        out_shape=out_shape,
        in_specs=[pl.BlockSpec(memory_space=space) for space in spaces],
        compiler_params=pltpu.CompilerParams(vmem_limit_bytes=LIMIT),
    )(*args)


def send_body(which, counts_ref, loading_ref, offset_ref, out_ref, held, row, sems):
    rows, comps = held.shape
    half = rows // 2
    copies = [
        pltpu.make_async_copy(
            counts_ref.at[pl.ds(pl.multiple_of(which[0] * rows + k * half, half), half), :],
            held.at[pl.ds(k * half, half), :],
            sems.at[k],
        )
        for k in range(2)
    ]
    copies.append(pltpu.make_async_copy(loading_ref, out_ref.at[pl.ds(rows, comps), :], sems.at[2]))
    copies.append(pltpu.make_async_copy(offset_ref, row, sems.at[3]))
    for copy in copies:
        copy.start()
    for k in range(2):
        copies[k].wait()
        out_ref[k * half : (k + 1) * half, :] = jnp.log(held[k * half : (k + 1) * half, :])
    copies[2].wait()
    copies[3].wait()
    out_ref[rows + comps : rows + comps + 8, :] = jnp.broadcast_to(row[...], (8, comps))


def keep_body(which, counts_ref, out_ref, held, sem):
    rows = held.shape[0]
    copy = pltpu.make_async_copy(
        counts_ref.at[pl.ds(pl.multiple_of(which[0] * rows, rows), rows), :], held, sem
    )
    copy.start()
    copy.wait()
    out_ref[...] = jnp.log(held[...])


def cut(body, height, scratch, which, counts, *more):
    rows, width = counts.shape[0] // 2, counts.shape[1]
    return pl.pallas_call(
        body,
        out_shape=whole(height, width),
        in_specs=[pl.BlockSpec(memory_space=pltpu.SMEM)]
        + [pl.BlockSpec(memory_space=pltpu.HBM)] * (1 + len(more)),
        scratch_shapes=[pltpu.VMEM((rows, width), F32)] + scratch,
        compiler_params=pltpu.CompilerParams(vmem_limit_bytes=LIMIT),
    )(which.reshape(1), *(pltpu.with_memory_space_constraint(a, pltpu.HBM) for a in (counts,) + more))


def fold(gram):
    half = gram.shape[0] // 2
    row = lax.broadcasted_iota(jnp.int32, (half, 2 * half), 0)
    col = lax.broadcasted_iota(jnp.int32, (half, 2 * half), 1)
    low = pltpu.roll(gram[half:, :], half, 1)
    folded = jnp.where((col < half) & (col > row), low, gram[:half, :])
    return folded, jnp.sum(jnp.where(col == row, low, 0.0), axis=0, keepdims=True)


def unfold(folded, diagonal):
    half = folded.shape[0]
    row = lax.broadcasted_iota(jnp.int32, (half, 2 * half), 0)
    col = lax.broadcasted_iota(jnp.int32, (half, 2 * half), 1)
    turned = jnp.concatenate([folded, jnp.zeros_like(folded)], axis=0).T
    high = jnp.where((col < half) & (col > row), turned[:half, :], folded)
    right = jnp.where(
        col - half > row,
        pltpu.roll(folded, half, 1),
        pltpu.roll(jnp.where(col == row, diagonal, turned[:half, :]), half, 1),
    )
    return jnp.concatenate([high, jnp.where(col < half, turned[half:, :], right)], axis=0)


def source_terms(load, off):
    bar = jnp.sum(load, axis=0, keepdims=True) / load.shape[0]
    return bar, load - bar, mult(off, load)[0:1, :], fold(mult(load, load, ((0,), (0,))))


def log_sums(logs):
    comps = logs.shape[1]
    return [
        jnp.sum(logs[h * comps : (h + 1) * comps, :].T, axis=0, keepdims=True)
        for h in range(logs.shape[0] // comps)
    ]


def encode_body(mine, loading_ref, offset_ref, out_ref):
    total, comps = mine.shape
    rows, share = total // PARTS, comps // 2 // PARTS
    bar, bare, shift, (gram, diagonal) = source_terms(
        loading_ref[...], jnp.broadcast_to(offset_ref[...], (8, comps))
    )
    blank = jnp.zeros((1, comps), F32)
    for j in range(PARTS):
        logs = mine[j * rows : (j + 1) * rows, :]
        out_ref[j, 0:rows, :] = mult(logs, bare)
        out_ref[j, rows : rows + 8, :] = jnp.concatenate(
            log_sums(logs) + [blank, blank, bar, blank, shift, diagonal], axis=0
        )
        out_ref[j, rows + 8 : rows + 8 + share, :] = gram[j * share : (j + 1) * share, :]


def encode_last_body(in_ref, other, out_ref):
    height, comps = in_ref.shape[1:]
    share = comps // 2 // PARTS
    rows = height - 8 - share
    total = PARTS * rows
    bar, bare, shift, (gram, diagonal) = source_terms(
        other[total : total + comps, :], other[total + comps : total + comps + 8, :]
    )
    blank = jnp.zeros((1, comps), F32)
    for j in range(PARTS):
        logs = other[j * rows : (j + 1) * rows, :]
        out_ref[j, 0:rows, :] = in_ref[j, 0:rows, :] + mult(logs, bare)
        out_ref[j, rows : rows + 8, :] = in_ref[j, rows : rows + 8, :] + jnp.concatenate(
            [blank, blank] + log_sums(logs) + [blank, bar, shift, diagonal], axis=0
        )
        at = rows + 8
        out_ref[j, at : at + share, :] = in_ref[j, at : at + share, :] + gram[j * share : (j + 1) * share, :]


def finish_body(channels, in_ref, out_ref):
    height, comps = in_ref.shape[1:]
    share = comps // 2 // PARTS
    rows = height - 8 - share
    group = channels // (2 * PARTS)
    bars = jnp.concatenate([in_ref[j, rows + 4 : rows + 6, :] for j in range(PARTS)], axis=0)
    shift = sum(in_ref[j, rows + 6 : rows + 7, :] for j in range(PARTS))
    geos = []
    for h in range(2):
        sums = jnp.concatenate(
            [
                in_ref[j, rows + h + k : rows + h + k + 1, :]
                for j in range(PARTS)
                for k in (0, 2)
            ],
            axis=0,
        )
        geo = jnp.sum(sums, axis=0, keepdims=True) / channels
        at = h * comps
        total = mult(sums - group * geo, bars, ((0,), (0,))) - shift
        for j in range(PARTS):
            total += in_ref[j, at : at + comps, :]
        out_ref[at : at + comps, :] = total
        geos.append(geo)
    diagonal = sum(in_ref[j, rows + 7 : rows + 8, :] for j in range(PARTS))
    out_ref[rows : rows + 8, :] = jnp.concatenate(geos + [diagonal, jnp.zeros((5, comps), F32)], axis=0)
    out_ref[rows + 8 : rows + 8 + share, :] = sum(in_ref[j, rows + 8 : rows + 8 + share, :] for j in range(PARTS))


def block_terms(first, flip, in_ref, logs, offs):
    blocks, height, comps = in_ref.shape
    rows = height - 8 - comps // 2 // PARTS
    wide, sums = 0.0, 0.0
    for j in range(blocks):
        s = in_ref[j, 0:rows, :]
        geo = jnp.concatenate(
            [
                jnp.broadcast_to(in_ref[j, rows + h : rows + h + 1, :], (comps, comps)).T
                for h in range(2)
            ],
            axis=0,
        )
        here = pl.ds(pl.multiple_of((2 * (j ^ flip) + first) * rows, rows), rows)
        both = jnp.concatenate([a[here, :] - geo - off for a, off in zip(logs, offs)] + [s], axis=1)
        sums += jnp.sum(both, axis=0, keepdims=True)
        wide += mult(s.T, both)
    return wide, sums


def some_grad_body(side, in_ref, mine, other, offset_ref, out_ref):
    total, comps = mine.shape
    offs = (offset_ref[...], other[total + comps : total + comps + 1, :])
    wide, sums = block_terms(side[0], side[1], in_ref, (mine, other), offs)
    out_ref[0:comps, :] = wide
    out_ref[comps : comps + 8, :] = jnp.broadcast_to(sums, (8, sums.shape[1]))


def grad_body(side, near_ref, in_ref, some_ref, mine, other, offset_ref, out_ref, rest_ref):
    total, comps = mine.shape
    height = in_ref.shape[1]
    share = comps // 2 // PARTS
    rows = height - 8 - share
    offs = (offset_ref[...], other[total + comps : total + comps + 1, :])
    wide, sums = block_terms(1 - side[0], side[1], near_ref, (mine, other), offs)
    wide, sums = wide + some_ref[0:comps, :], sums + some_ref[comps : comps + 1, :]
    def whole_gram(order):
        shares = [[a[j, rows + 8 : rows + 8 + share, :] for a in (in_ref, near_ref)] for j in order]
        here = jnp.concatenate([a for pair in shares for a in pair], axis=0)
        there = jnp.concatenate([a for pair in shares for a in pair[::-1]], axis=0)
        return jnp.where(side[0] == 0, here, there)

    order = list(range(PARTS // 2))
    gram = jnp.where(side[1] == 0, whole_gram(order), whole_gram(order[::-1]))
    gram = unfold(gram, in_ref[0, rows + 2 : rows + 3, :])
    row = lax.broadcasted_iota(jnp.int32, (comps, comps), 0)
    col = lax.broadcasted_iota(jnp.int32, (comps, comps), 1)
    hat = gram - jnp.where(row == col, 2.0, 0.0).astype(F32)
    square = wide[:, 2 * comps : 3 * comps]
    s_sum, c_mine, c_other = (sums[:, k * comps : (k + 1) * comps] for k in (2, 0, 1))
    source_grad(wide[:, comps : 2 * comps], hat, square, s_sum, c_other, other[total : total + comps, :], out_ref)
    rest_ref[0] = wide[:, 0:comps]
    rest_ref[1] = hat
    rest_ref[2] = square
    rest_ref[3] = jnp.broadcast_to(s_sum, (comps, comps))
    rest_ref[4] = jnp.broadcast_to(c_mine, (comps, comps))


def source_grad(w_turned, hat, square, s_sum, c_sum, load, out_ref):
    comps = load.shape[1]
    s_hat = mult(jnp.broadcast_to(s_sum, (8, comps)), hat)
    out_ref[0:comps, :] = mult(w_turned, hat, ((0,), (0,))) + mult(load, square)
    out_ref[comps : comps + 8, :] = -(mult(s_hat, load, ((1,), (1,))) + c_sum)


def mine_grad_body(rest_ref, loading_ref, out_ref):
    source_grad(
        rest_ref[0], rest_ref[1], rest_ref[2], rest_ref[3, 0:1, :], rest_ref[4, 0:1, :], loading_ref[...], out_ref
    )


def deal_body(a_ref, b_ref, out_ref):
    pieces, _, comps = out_ref.shape
    share = comps // pieces
    total = a_ref[...] + b_ref[...]
    for p in range(pieces):
        out_ref[p, 0:share, :] = total[p * share : (p + 1) * share, :]
        out_ref[p, share:8, :] = total[comps : comps + 8 - share, :]


def gather_body(pixels, in_ref, out_ref):
    total = jnp.sum(in_ref[...], axis=0) / pixels
    for j in range(out_ref.shape[0]):
        out_ref[j] = total


def last_body(in_ref, load_ref, off_ref):
    pieces = in_ref.shape[0]
    share = load_ref.shape[0] // pieces
    for p in range(pieces):
        load_ref[p * share : (p + 1) * share, :] = in_ref[p, 0:share, :]
    off_ref[...] = in_ref[0, share : share + 1, :]


def on_device(counts, offset, loading):
    pixels = counts.shape[0] * lax.axis_size(WIDE)
    comps = loading.shape[1]
    channels = counts.shape[1] * PARTS * 2
    height = counts.shape[0] // 2 // PARTS + 8 + comps // 2 // PARTS
    core = lax.axis_index("c").astype(jnp.int32)
    side = jnp.stack([lax.axis_index("zl").astype(jnp.int32), (PARTS // 2 - 1) * core])
    offset = offset.reshape(1, comps)

    swap = [(0, 1), (1, 0)]
    near_pairs = []
    for z in range(PARTS):
        for c in range(2):
            partner = (((z - c) % PARTS ^ 1) + c) % PARTS
            near_pairs.append((2 * z + c, 2 * partner + c))

    quads = [[2 * z + c for z in range(k, PARTS, 2)][:: 1 - 2 * c] for c in range(2) for k in range(2)]
    plane = lax.axis_size(WIDE)
    planes = [
        [2 * (PARTS * p + z) + c for p in (reversed(range(plane)) if c else range(plane))]
        for z in range(PARTS)
        for c in range(2)
    ]

    half = counts.shape[0] // 2
    scratch = [pltpu.VMEM((1, comps), F32), pltpu.SemaphoreType.DMA((4,))]
    sent = cut(send_body, half + comps + 8, scratch, 1 - core, counts, loading, offset)
    other = lax.ppermute(sent, "c", swap)
    mine = cut(keep_body, half, [pltpu.SemaphoreType.DMA], core, counts)
    block = whole(PARTS, height, comps)
    partial = call(encode_body, block, mine, loading, offset)
    partial = call(encode_last_body, block, partial, other)
    gathered = lax.all_to_all(partial, ("zh", "zl"), 0, 0)
    own = call(functools.partial(finish_body, channels), whole(height, comps), gathered)
    scores = lax.all_gather(own, DEEP, axis=0, axis_index_groups=quads)
    near = lax.ppermute(scores, DEEP, near_pairs)
    some = call(
        some_grad_body, whole(comps + 8, 3 * comps), side, scores, mine, other, offset, scalars=1
    )
    shape = whole(comps + 8, comps)
    grad_other, rest = call(
        grad_body, (shape, whole(5, comps, comps)), side, near, scores, some, mine, other, offset, scalars=1
    )
    arrived = lax.ppermute(grad_other, "c", swap)
    grad_mine = call(mine_grad_body, shape, rest, loading)
    pieces = call(deal_body, whole(plane, 8, comps), grad_mine, arrived)
    pieces = lax.all_to_all(pieces, AXES, 0, 0, axis_index_groups=planes)
    pieces = call(functools.partial(gather_body, pixels), whole(plane, 8, comps), pieces)
    pieces = lax.all_to_all(pieces, AXES, 0, 0, axis_index_groups=planes)
    grad, grad_offset = call(last_body, (whole(comps, comps), whole(1, comps)), pieces)
    return grad, grad_offset.reshape(comps)


def solution(mesh):
    wide, deep = mesh.devices.shape
    split_mesh = Mesh(mesh.devices.reshape(wide // 4, 4, deep // 4, 2, 2), AXES)
    return jax.shard_map(
        on_device,
        mesh=split_mesh,
        in_specs=(P(WIDE, DEEP), P(DEEP), P(DEEP, None)),
        out_specs=(P(DEEP, None), P(DEEP)),
        check_vma=False,
    )
```

```python
import functools

import jax
import jax.numpy as jnp
from jax import lax
from jax.experimental import pallas as pl
from jax.experimental.pallas import tpu as pltpu
from jax.sharding import Mesh
from jax.sharding import PartitionSpec as P

F32 = jnp.float32
AXES = ("y", "x", "zh", "zl", "c")
WIDE = ("y", "x")
DEEP = ("zh", "zl", "c")
PARTS = 8
LIMIT = 48 * 1024 * 1024


def mult(left, right, contract=((1,), (0,))):
    return lax.dot_general(
        left, right, (contract, ((), ())),
        preferred_element_type=F32, precision=lax.Precision.HIGHEST,
    )


def whole(*shape):
    return jax.ShapeDtypeStruct(shape, F32)


def call(body, out_shape, *args, scalars=0):
    spaces = [pltpu.SMEM] * scalars + [pltpu.VMEM] * (len(args) - scalars)
    return pl.pallas_call(
        body,
        out_shape=out_shape,
        in_specs=[pl.BlockSpec(memory_space=space) for space in spaces],
        compiler_params=pltpu.CompilerParams(vmem_limit_bytes=LIMIT),
    )(*args)


def send_body(which, counts_ref, loading_ref, offset_ref, out_ref, held, row, sems):
    rows, comps = held.shape
    half = rows // 2
    copies = [
        pltpu.make_async_copy(
            counts_ref.at[pl.ds(pl.multiple_of(which[0] * rows + k * half, half), half), :],
            held.at[pl.ds(k * half, half), :],
            sems.at[k],
        )
        for k in range(2)
    ]
    copies.append(pltpu.make_async_copy(loading_ref, out_ref.at[pl.ds(rows, comps), :], sems.at[2]))
    copies.append(pltpu.make_async_copy(offset_ref, row, sems.at[3]))
    for copy in copies:
        copy.start()
    for k in range(2):
        copies[k].wait()
        out_ref[k * half : (k + 1) * half, :] = jnp.log(held[k * half : (k + 1) * half, :])
    copies[2].wait()
    copies[3].wait()
    out_ref[rows + comps : rows + comps + 8, :] = jnp.broadcast_to(row[...], (8, comps))


def keep_body(which, counts_ref, out_ref, held, sem):
    rows = held.shape[0]
    copy = pltpu.make_async_copy(
        counts_ref.at[pl.ds(pl.multiple_of(which[0] * rows, rows), rows), :], held, sem
    )
    copy.start()
    copy.wait()
    out_ref[...] = jnp.log(held[...])


def cut(body, height, scratch, which, counts, *more):
    rows, width = counts.shape[0] // 2, counts.shape[1]
    return pl.pallas_call(
        body,
        out_shape=whole(height, width),
        in_specs=[pl.BlockSpec(memory_space=pltpu.SMEM)]
        + [pl.BlockSpec(memory_space=pltpu.HBM)] * (1 + len(more)),
        scratch_shapes=[pltpu.VMEM((rows, width), F32)] + scratch,
        compiler_params=pltpu.CompilerParams(vmem_limit_bytes=LIMIT),
    )(which.reshape(1), *(pltpu.with_memory_space_constraint(a, pltpu.HBM) for a in (counts,) + more))


def fold(gram):
    half = gram.shape[0] // 2
    row = lax.broadcasted_iota(jnp.int32, (half, 2 * half), 0)
    col = lax.broadcasted_iota(jnp.int32, (half, 2 * half), 1)
    low = pltpu.roll(gram[half:, :], half, 1)
    folded = jnp.where((col < half) & (col > row), low, gram[:half, :])
    return folded, jnp.sum(jnp.where(col == row, low, 0.0), axis=0, keepdims=True)


def unfold(folded, diagonal):
    half = folded.shape[0]
    row = lax.broadcasted_iota(jnp.int32, (half, 2 * half), 0)
    col = lax.broadcasted_iota(jnp.int32, (half, 2 * half), 1)
    turned = jnp.concatenate([folded, jnp.zeros_like(folded)], axis=0).T
    high = jnp.where((col < half) & (col > row), turned[:half, :], folded)
    right = jnp.where(
        col - half > row,
        pltpu.roll(folded, half, 1),
        pltpu.roll(jnp.where(col == row, diagonal, turned[:half, :]), half, 1),
    )
    return jnp.concatenate([high, jnp.where(col < half, turned[half:, :], right)], axis=0)


def source_terms(load, off):
    bar = jnp.sum(load, axis=0, keepdims=True) / load.shape[0]
    return bar, load - bar, mult(off, load)[0:1, :], fold(mult(load, load, ((0,), (0,))))


def log_sums(logs):
    comps = logs.shape[1]
    return [
        jnp.sum(logs[h * comps : (h + 1) * comps, :].T, axis=0, keepdims=True)
        for h in range(logs.shape[0] // comps)
    ]


def encode_body(mine, loading_ref, offset_ref, out_ref):
    total, comps = mine.shape
    rows, share = total // PARTS, comps // 2 // PARTS
    bar, bare, shift, (gram, diagonal) = source_terms(
        loading_ref[...], jnp.broadcast_to(offset_ref[...], (8, comps))
    )
    blank = jnp.zeros((1, comps), F32)
    for j in range(PARTS):
        logs = mine[j * rows : (j + 1) * rows, :]
        out_ref[j, 0:rows, :] = mult(logs, bare)
        out_ref[j, rows : rows + 8, :] = jnp.concatenate(
            log_sums(logs) + [blank, blank, bar, blank, shift, diagonal], axis=0
        )
        out_ref[j, rows + 8 : rows + 8 + share, :] = gram[j * share : (j + 1) * share, :]


def encode_last_body(in_ref, other, out_ref):
    height, comps = in_ref.shape[1:]
    share = comps // 2 // PARTS
    rows = height - 8 - share
    total = PARTS * rows
    bar, bare, shift, (gram, diagonal) = source_terms(
        other[total : total + comps, :], other[total + comps : total + comps + 8, :]
    )
    blank = jnp.zeros((1, comps), F32)
    for j in range(PARTS):
        logs = other[j * rows : (j + 1) * rows, :]
        out_ref[j, 0:rows, :] = in_ref[j, 0:rows, :] + mult(logs, bare)
        out_ref[j, rows : rows + 8, :] = in_ref[j, rows : rows + 8, :] + jnp.concatenate(
            [blank, blank] + log_sums(logs) + [blank, bar, shift, diagonal], axis=0
        )
        at = rows + 8
        out_ref[j, at : at + share, :] = in_ref[j, at : at + share, :] + gram[j * share : (j + 1) * share, :]


def finish_body(channels, in_ref, out_ref):
    height, comps = in_ref.shape[1:]
    share = comps // 2 // PARTS
    rows = height - 8 - share
    group = channels // (2 * PARTS)
    bars = jnp.concatenate([in_ref[j, rows + 4 : rows + 6, :] for j in range(PARTS)], axis=0)
    shift = sum(in_ref[j, rows + 6 : rows + 7, :] for j in range(PARTS))
    geos = []
    for h in range(2):
        sums = jnp.concatenate(
            [
                in_ref[j, rows + h + k : rows + h + k + 1, :]
                for j in range(PARTS)
                for k in (0, 2)
            ],
            axis=0,
        )
        geo = jnp.sum(sums, axis=0, keepdims=True) / channels
        at = h * comps
        total = mult(sums - group * geo, bars, ((0,), (0,))) - shift
        for j in range(PARTS):
            total += in_ref[j, at : at + comps, :]
        out_ref[at : at + comps, :] = total
        geos.append(geo)
    diagonal = sum(in_ref[j, rows + 7 : rows + 8, :] for j in range(PARTS))
    out_ref[rows : rows + 8, :] = jnp.concatenate(geos + [diagonal, jnp.zeros((5, comps), F32)], axis=0)
    out_ref[rows + 8 : rows + 8 + share, :] = sum(in_ref[j, rows + 8 : rows + 8 + share, :] for j in range(PARTS))


def block_terms(first, in_ref, logs, offs):
    blocks, height, comps = in_ref.shape
    rows = height - 8 - comps // 2 // PARTS
    wide, sums = 0.0, 0.0
    for j in range(blocks):
        s = in_ref[j, 0:rows, :]
        geo = jnp.concatenate(
            [
                jnp.broadcast_to(in_ref[j, rows + h : rows + h + 1, :], (comps, comps)).T
                for h in range(2)
            ],
            axis=0,
        )
        here = pl.ds(pl.multiple_of((2 * j + first) * rows, rows), rows)
        both = jnp.concatenate([a[here, :] - geo - off for a, off in zip(logs, offs)] + [s], axis=1)
        sums += jnp.sum(both, axis=0, keepdims=True)
        wide += mult(s.T, both)
    return wide, sums


def some_grad_body(side, in_ref, mine, other, offset_ref, out_ref):
    total, comps = mine.shape
    offs = (offset_ref[...], other[total + comps : total + comps + 1, :])
    wide, sums = block_terms(side[0], in_ref, (mine, other), offs)
    out_ref[0:comps, :] = wide
    out_ref[comps : comps + 8, :] = jnp.broadcast_to(sums, (8, sums.shape[1]))


def grad_body(side, near_ref, in_ref, some_ref, mine, other, offset_ref, out_ref, rest_ref):
    total, comps = mine.shape
    height = in_ref.shape[1]
    share = comps // 2 // PARTS
    rows = height - 8 - share
    offs = (offset_ref[...], other[total + comps : total + comps + 1, :])
    wide, sums = block_terms(1 - side[0], near_ref, (mine, other), offs)
    wide, sums = wide + some_ref[0:comps, :], sums + some_ref[comps : comps + 1, :]
    here = [a[j, rows + 8 : rows + 8 + share, :] for j in range(PARTS // 2) for a in (in_ref, near_ref)]
    there = [a[j, rows + 8 : rows + 8 + share, :] for j in range(PARTS // 2) for a in (near_ref, in_ref)]
    gram = jnp.where(side[0] == 0, jnp.concatenate(here, axis=0), jnp.concatenate(there, axis=0))
    gram = unfold(gram, in_ref[0, rows + 2 : rows + 3, :])
    row = lax.broadcasted_iota(jnp.int32, (comps, comps), 0)
    col = lax.broadcasted_iota(jnp.int32, (comps, comps), 1)
    hat = gram - jnp.where(row == col, 2.0, 0.0).astype(F32)
    square = wide[:, 2 * comps : 3 * comps]
    s_sum, c_mine, c_other = (sums[:, k * comps : (k + 1) * comps] for k in (2, 0, 1))
    source_grad(wide[:, comps : 2 * comps], hat, square, s_sum, c_other, other[total : total + comps, :], out_ref)
    rest_ref[0] = wide[:, 0:comps]
    rest_ref[1] = hat
    rest_ref[2] = square
    rest_ref[3] = jnp.broadcast_to(s_sum, (comps, comps))
    rest_ref[4] = jnp.broadcast_to(c_mine, (comps, comps))


def source_grad(w_turned, hat, square, s_sum, c_sum, load, out_ref):
    comps = load.shape[1]
    s_hat = mult(jnp.broadcast_to(s_sum, (8, comps)), hat)
    out_ref[0:comps, :] = mult(w_turned, hat, ((0,), (0,))) + mult(load, square)
    out_ref[comps : comps + 8, :] = -(mult(s_hat, load, ((1,), (1,))) + c_sum)


def mine_grad_body(rest_ref, loading_ref, out_ref):
    source_grad(
        rest_ref[0], rest_ref[1], rest_ref[2], rest_ref[3, 0:1, :], rest_ref[4, 0:1, :], loading_ref[...], out_ref
    )


def deal_body(a_ref, b_ref, out_ref):
    pieces, _, comps = out_ref.shape
    share = comps // pieces
    total = a_ref[...] + b_ref[...]
    for p in range(pieces):
        out_ref[p, 0:share, :] = total[p * share : (p + 1) * share, :]
        out_ref[p, share:8, :] = total[comps : comps + 8 - share, :]


def gather_body(pixels, in_ref, out_ref):
    total = jnp.sum(in_ref[...], axis=0) / pixels
    for j in range(out_ref.shape[0]):
        out_ref[j] = total


def last_body(in_ref, load_ref, off_ref):
    pieces = in_ref.shape[0]
    share = load_ref.shape[0] // pieces
    for p in range(pieces):
        load_ref[p * share : (p + 1) * share, :] = in_ref[p, 0:share, :]
    off_ref[...] = in_ref[0, share : share + 1, :]


def on_device(counts, offset, loading):
    pixels = counts.shape[0] * lax.axis_size(WIDE)
    comps = loading.shape[1]
    channels = counts.shape[1] * PARTS * 2
    height = counts.shape[0] // 2 // PARTS + 8 + comps // 2 // PARTS
    core = lax.axis_index("c").astype(jnp.int32)
    side = lax.axis_index("zl").astype(jnp.int32).reshape(1)
    offset = offset.reshape(1, comps)

    swap = [(0, 1), (1, 0)]
    near_pairs = []
    for z in range(PARTS):
        for c in range(2):
            partner = (((z - c) % PARTS ^ 1) + c) % PARTS
            near_pairs.append((2 * z + c, 2 * partner + c))

    rings = [[2 * (step * k % PARTS) + c for k in range(PARTS)] for c, step in ((0, 3), (1, PARTS - 3))]
    rings4 = [ring[k::2] for ring in rings for k in range(2)]
    plane = lax.axis_size(WIDE)
    planes = [
        [2 * (PARTS * p + z) + c for p in (reversed(range(plane)) if c else range(plane))]
        for z in range(PARTS)
        for c in range(2)
    ]

    half = counts.shape[0] // 2
    scratch = [pltpu.VMEM((1, comps), F32), pltpu.SemaphoreType.DMA((4,))]
    sent = cut(send_body, half + comps + 8, scratch, 1 - core, counts, loading, offset)
    other = lax.ppermute(sent, "c", swap)
    mine = cut(keep_body, half, [pltpu.SemaphoreType.DMA], core, counts)
    block = whole(PARTS, height, comps)
    partial = call(encode_body, block, mine, loading, offset)
    partial = call(encode_last_body, block, partial, other)
    gathered = lax.all_to_all(partial, DEEP, 0, 0, axis_index_groups=rings)
    own = call(functools.partial(finish_body, channels), whole(height, comps), gathered)
    scores = lax.all_gather(own, DEEP, axis=0, axis_index_groups=rings4)
    near = lax.ppermute(scores, DEEP, near_pairs)
    some = call(
        some_grad_body, whole(comps + 8, 3 * comps), side, scores, mine, other, offset, scalars=1
    )
    shape = whole(comps + 8, comps)
    grad_other, rest = call(
        grad_body, (shape, whole(5, comps, comps)), side, near, scores, some, mine, other, offset, scalars=1
    )
    arrived = lax.ppermute(grad_other, "c", swap)
    grad_mine = call(mine_grad_body, shape, rest, loading)
    pieces = call(deal_body, whole(plane, 8, comps), grad_mine, arrived)
    pieces = lax.all_to_all(pieces, AXES, 0, 0, axis_index_groups=planes)
    pieces = call(functools.partial(gather_body, pixels), whole(plane, 8, comps), pieces)
    pieces = lax.all_to_all(pieces, AXES, 0, 0, axis_index_groups=planes)
    grad, grad_offset = call(last_body, (whole(comps, comps), whole(1, comps)), pieces)
    return grad, grad_offset.reshape(comps)


def solution(mesh):
    wide, deep = mesh.devices.shape
    split_mesh = Mesh(mesh.devices.reshape(wide // 4, 4, deep // 4, 2, 2), AXES)
    return jax.shard_map(
        on_device,
        mesh=split_mesh,
        in_specs=(P(WIDE, DEEP), P(DEEP), P(DEEP, None)),
        out_specs=(P(DEEP, None), P(DEEP)),
        check_vma=False,
    )
```
